128 devices in a mesh: dp: 8 (over x, core), mp: 16 (over z, y).
Axes of the slice: x: 4, y: 4, z: 4, core: 2. Of those that a mesh axis runs over, the one named last changes fastest.
Arguments:
- gradient: float32 [8, 1024, 5120], P('dp', 'mp'), may hold values from -40 to 40
- feedback: float32 [8, 1024, 5120], P('dp', 'mp'), may hold values from -3 to 3
- q_previous: float32 [16, 5120], replicated, may hold values from -6 to 6
Outputs:
- new_feedback: float32 [8, 1024, 5120], P('dp', 'mp')
- p_ortho: float32 [16, 1024], P(None, 'mp')
- q_factor: float32 [16, 5120], replicated
The draws below stay inside these ranges and needn't reach their ends.
All inputs are finite; a program needn't handle non-finite values.
Results may differ from the reference program's by a relative error of at most 0.000075.
Values sent between devices are 32-bit elements; how exact they have to be, the bound alone decides.
No kernel may reach another device: no remote copies, remote signals or barrier semaphores. Data moves between devices by JAX's collectives and lax.ppermute only.
A program may use at most 64 MiB of HBM per device.

```python
import jax
import jax.numpy as jnp
from jax import lax

D = 5120
RANK = 16
ROWS = 1024
N_DP = 8


def draw_gradient(key, part):
    key = jax.random.fold_in(key, 7)
    k_common, k_rows, k_cols, k_rep, k_scale = jax.random.split(key, 5)
    row_scale = jnp.exp(jax.random.uniform(k_rows, (ROWS, 1), jnp.float32, -1.15, 1.15))
    col_scale = jnp.exp(jax.random.uniform(k_cols, (1, D), jnp.float32, -1.15, 1.15))
    rep_scale = jnp.exp(jax.random.uniform(k_scale, (N_DP, 1, 1), jnp.float32, -0.55, 0.55))
    common = jax.random.truncated_normal(k_common, -3.0, 3.0, (ROWS, D), jnp.float32)
    own = jax.random.truncated_normal(k_rep, -3.0, 3.0, (N_DP, ROWS, D), jnp.float32)
    shared = common * row_scale * col_scale
    return (shared[None] + own * rep_scale).astype(jnp.float32)


def shard_levels(own_key, extent, pieces, low, high):
    factor_of = 1.0
    for axis_at, shards_of in pieces:
        steps = jax.random.uniform(jax.random.fold_in(jax.random.fold_in(own_key, 6), axis_at), (shards_of,), jnp.float32, low / len(pieces), high / len(pieces))
        factor_of = factor_of * jnp.repeat(jnp.exp(steps), extent[axis_at] // shards_of).reshape((-1,) + (1,) * (len(extent) - 1 - axis_at))
    return factor_of


def scatter_about(own_key, shape, deviation, limit, pieces=(), dtype=jnp.bfloat16):
    array = deviation * jax.random.normal(own_key, shape, jnp.float32)
    if pieces:
        array = array * shard_levels(own_key, shape, pieces, -0.22, 0.18)
    return jnp.clip(array, -limit, limit).astype(dtype)


def setup_inputs(seed: int = 0) -> dict:
    keys = jax.random.split(jax.random.key(seed), 4)
    return {
        "gradient": draw_gradient(jax.random.fold_in(keys[3], 71), 0),
        "feedback": scatter_about(keys[1], (N_DP, ROWS, D), 0.5, 3.0, ((0, 8), (1, 16)), jnp.float32),
        "q_previous": scatter_about(keys[2], (RANK, D), 1.0, 6.0, (), jnp.float32),
    }


def reference(gradient, feedback, q_previous):
    hp = lax.Precision.HIGHEST
    corrected = gradient + feedback
    p_mean = jnp.einsum('kd,nrd->kr', q_previous, corrected, precision=hp) / N_DP
    gram = jnp.dot(p_mean, p_mean.T, precision=hp)
    lower = jnp.linalg.cholesky(gram)
    p_ortho = jax.scipy.linalg.solve_triangular(lower, p_mean, lower=True)
    q_factor = jnp.einsum('kr,nrd->kd', p_ortho, corrected, precision=hp) / N_DP
    update = jnp.dot(p_ortho.T, q_factor, precision=hp)
    new_feedback = corrected - update[None]
    return (new_feedback, p_ortho, q_factor)
```

```python
import functools

import jax
import jax.numpy as jnp
from jax import lax
from jax.experimental import pallas as pl
from jax.experimental.pallas import tpu as pltpu
from jax.sharding import PartitionSpec as P

LANES = 128
SUBLANES = 8
STEPS = 4


def dot(left, right, left_dim, right_dim):
    return lax.dot_general(
        left,
        right,
        (((left_dim,), (right_dim,)), ((), ())),
        precision=lax.Precision.HIGHEST,
        preferred_element_type=jnp.float32,
    )


def correct_kernel(g_ref, f_ref, q_ref, c_ref, p_ref, acc):
    step = pl.program_id(0)
    local = g_ref[0] + f_ref[0]
    c_ref[...] = local
    part = dot(q_ref[...], local, 1, 1)

    @pl.when(step == 0)
    def _():
        acc[...] = part

    @pl.when(step > 0)
    def _():
        acc[...] += part

    @pl.when(step == pl.num_programs(0) - 1)
    def _():
        half = acc.shape[0] // 2
        packed = jnp.concatenate([acc[:half], acc[half:]], axis=1)
        p_ref[...] = jnp.broadcast_to(packed[None], p_ref.shape)


def group_mask(rank):
    row = lax.broadcasted_iota(jnp.int32, (rank, LANES), 0)
    lane = lax.broadcasted_iota(jnp.int32, (rank, LANES), 1)
    return lane - rank * (row % SUBLANES)


def project_kernel(p_ref, c_ref, msg_ref, mean_ref):
    total = p_ref[0]
    for n in range(1, p_ref.shape[0]):
        total = total + p_ref[n]
    total = total * (1.0 / p_ref.shape[0])
    half = total.shape[1] // 2
    mean = jnp.concatenate([total[:, :half], total[:, half:]], axis=0)
    mean_ref[...] = mean
    rank = mean.shape[0]
    groups = SUBLANES
    width = c_ref.shape[1] // groups
    for j in range(groups):
        out = dot(mean, c_ref[:, j * width : (j + 1) * width], 1, 0)
        for i in range(width // LANES):
            msg_ref[pl.ds(j * SUBLANES + i, rank, stride=groups * SUBLANES), :] = out[:, i * LANES : (i + 1) * LANES]
    tiled = jnp.concatenate([mean] * (LANES // rank), axis=0)
    gram = dot(mean, tiled, 1, 1)
    at = group_mask(rank)
    gram = jnp.where((at >= 0) & (at < rank), gram, 0.0)
    peers = msg_ref.shape[0] // SUBLANES
    for h in range(rank // SUBLANES):
        line = jnp.sum(gram[h * SUBLANES : (h + 1) * SUBLANES], axis=0, keepdims=True)
        msg_ref[pl.ds(5 + h, peers, stride=SUBLANES), :] = jnp.broadcast_to(line, (peers, LANES))
    msg_ref[pl.ds(7, peers, stride=SUBLANES), :] = jnp.zeros((peers, LANES), jnp.float32)


def sum_kernel(in_ref, out_ref):
    out_ref[...] = jnp.broadcast_to(jnp.sum(in_ref[...], axis=0, keepdims=True), out_ref.shape)


def inverse_factor(lines, rank, replicas):
    spread = jnp.concatenate(
        [jnp.broadcast_to(lines[h : h + 1], (SUBLANES, LANES)) for h in range(rank // SUBLANES)], axis=0
    ) * (1.0 / replicas)
    at = group_mask(rank)
    row = lax.broadcasted_iota(jnp.int32, (rank, LANES), 0)
    lane = lax.broadcasted_iota(jnp.int32, (rank, LANES), 1)
    cols = [
        jnp.broadcast_to(jnp.sum(jnp.where(at == j, spread, 0.0), axis=1, keepdims=True), (rank, LANES))
        for j in range(rank)
    ]
    right = jnp.where(row == lane, 1.0, 0.0)
    pivots = jnp.ones((rank, LANES), jnp.float32)
    for k in range(rank):
        pivot = cols[k][k : k + 1]
        pivots = jnp.where(row == k, pivot, pivots)
        factor = jnp.where(row > k, cols[k] * (1.0 / pivot), 0.0)
        for j in range(k + 1, rank):
            cols[j] = cols[j] - factor * cols[j][k : k + 1]
        right = right - factor * right[k : k + 1]
    return right * (1.0 / jnp.sqrt(pivots))


def finish_kernel(replicas, own_ref, all_ref, mean_ref, c_ref, nf_ref, po_ref, qf_ref, inv, ortho):
    step = pl.program_id(0)
    rank = mean_ref.shape[0]

    @pl.when(step == 0)
    def _():
        whole = inverse_factor(own_ref[5:7, :], rank, replicas)
        inv[...] = whole
        ortho[...] = dot(whole[:, :rank], mean_ref[...], 1, 0)
        po_ref[...] = ortho[...]

    block = c_ref.shape[1]
    per_group = all_ref.shape[0] // rank // SUBLANES
    width = block * pl.num_programs(0) // per_group
    lower = inv[:, :rank]
    left = ortho[...]
    for jj in range(block // width):
        j = step * (block // width) + jj
        raw = jnp.concatenate(
            [
                all_ref[pl.ds(j * SUBLANES + i, rank, stride=per_group * SUBLANES), :]
                for i in range(width // LANES)
            ],
            axis=1,
        ) * (1.0 / replicas)
        factor = dot(lower, raw, 1, 0)
        cols = slice(jj * width, (jj + 1) * width)
        qf_ref[:, cols] = factor
        nf_ref[0, :, cols] = c_ref[:, cols] - dot(left, factor, 0, 0)


def body(gradient, feedback, q_previous):
    f32 = jnp.float32
    dp, mp = lax.axis_size("dp"), lax.axis_size("mp")
    _, rows, width = gradient.shape
    rank = q_previous.shape[0]
    block = width // STEPS
    peers = dp * mp
    vmem = pl.BlockSpec(memory_space=pltpu.VMEM)
    params = pltpu.CompilerParams(vmem_limit_bytes=16 * 2**20)

    local, p_out = pl.pallas_call(
        correct_kernel,
        grid=(STEPS,),
        in_specs=[
            pl.BlockSpec((1, rows, block), lambda i: (0, 0, i)),
            pl.BlockSpec((1, rows, block), lambda i: (0, 0, i)),
            pl.BlockSpec((rank, block), lambda i: (0, i)),
        ],
        out_specs=[
            pl.BlockSpec((rows, block), lambda i: (0, i)),
            pl.BlockSpec((dp, rank // 2, 2 * rows), lambda i: (0, 0, 0)),
        ],
        out_shape=[
            jax.ShapeDtypeStruct((rows, width), f32),
            jax.ShapeDtypeStruct((dp, rank // 2, 2 * rows), f32),
        ],
        scratch_shapes=[pltpu.VMEM((rank, rows), f32)],
        compiler_params=params,
        name="correct",
    )(gradient, feedback, q_previous)
    p_all = lax.all_to_all(p_out, "dp", 0, 0, tiled=True)

    msg, p_mean = pl.pallas_call(
        project_kernel,
        in_specs=[vmem, vmem],
        out_specs=[vmem, vmem],
        out_shape=[
            jax.ShapeDtypeStruct((peers * SUBLANES, LANES), f32),
            jax.ShapeDtypeStruct((rank, rows), f32),
        ],
        compiler_params=params,
        name="project",
    )(p_all, local)
    terms = lax.all_to_all(msg.reshape(peers, SUBLANES, LANES), ("dp", "mp"), 0, 0, tiled=True)

    own = pl.pallas_call(
        sum_kernel,
        in_specs=[vmem],
        out_specs=vmem,
        out_shape=jax.ShapeDtypeStruct((peers, SUBLANES, LANES), f32),
        compiler_params=params,
        name="sum_terms",
    )(terms)
    whole = lax.all_to_all(own, ("dp", "mp"), 0, 0, tiled=True)

    new_feedback, p_ortho, q_factor = pl.pallas_call(
        functools.partial(finish_kernel, dp),
        grid=(STEPS,),
        in_specs=[
            pl.BlockSpec((SUBLANES, LANES), lambda i: (0, 0)),
            pl.BlockSpec((peers * SUBLANES, LANES), lambda i: (0, 0)),
            pl.BlockSpec((rank, rows), lambda i: (0, 0)),
            pl.BlockSpec((rows, block), lambda i: (0, i)),
        ],
        out_specs=[
            pl.BlockSpec((1, rows, block), lambda i: (0, 0, i)),
            pl.BlockSpec((rank, rows), lambda i: (0, 0)),
            pl.BlockSpec((rank, block), lambda i: (0, i)),
        ],
        out_shape=[
            jax.ShapeDtypeStruct((1, rows, width), f32),
            jax.ShapeDtypeStruct((rank, rows), f32),
            jax.ShapeDtypeStruct((rank, width), f32),
        ],
        scratch_shapes=[pltpu.VMEM((rank, LANES), f32), pltpu.VMEM((rank, rows), f32)],
        compiler_params=params,
        name="finish",
    )(own.reshape(peers * SUBLANES, LANES), whole.reshape(peers * SUBLANES, LANES), p_mean, local)
    return (new_feedback, p_ortho, q_factor)


def solution(mesh):
    return jax.shard_map(
        body,
        mesh=mesh,
        in_specs=(P("dp", "mp", None), P("dp", "mp", None), P()),
        out_specs=(P("dp", "mp", None), P(None, "mp"), P()),
        check_vma=False,
    )
```

```python
import functools

import jax
import jax.numpy as jnp
from jax import lax
from jax.experimental import pallas as pl
from jax.experimental.pallas import tpu as pltpu
from jax.sharding import PartitionSpec as P

LANES = 128
IN_PARTS = 5
GROUPS = 8


def dot(left, right, left_dim, right_dim):
    return lax.dot_general(
        left,
        right,
        (((left_dim,), (right_dim,)), ((), ())),
        precision=lax.Precision.HIGHEST,
        preferred_element_type=jnp.float32,
    )


def correct_kernel(g_hbm, f_hbm, q_hbm, p_ref, g_buf, f_buf, q_buf, sems):
    width = g_buf.shape[1] // IN_PARTS
    copies = []
    for s in range(IN_PARTS):
        cols = pl.ds(s * width, width)
        part = [
            pltpu.make_async_copy(g_hbm.at[0, :, cols], g_buf.at[:, cols], sems.at[0, s]),
            pltpu.make_async_copy(f_hbm.at[0, :, cols], f_buf.at[:, cols], sems.at[1, s]),
            pltpu.make_async_copy(q_hbm.at[:, cols], q_buf.at[:, cols], sems.at[2, s]),
        ]
        for copy in part:
            copy.start()
        copies.append(part)
    total = None
    for s in range(IN_PARTS):
        for copy in copies[s]:
            copy.wait()
        cols = slice(s * width, (s + 1) * width)
        local = g_buf[:, cols] + f_buf[:, cols]
        part = dot(q_buf[:, cols], local, 1, 1)
        total = part if total is None else total + part
    half = total.shape[0] // 2
    packed = jnp.concatenate([total[:half], total[half:]], axis=1)
    p_ref[...] = jnp.broadcast_to(packed[None], p_ref.shape)


def project_kernel(p_ref, g_ref, f_ref, msg_ref, mean_ref, c_ref):
    replicas = p_ref.shape[0]
    total = p_ref[0]
    for n in range(1, replicas):
        total = total + p_ref[n]
    total = total * (1.0 / replicas)
    half = total.shape[1] // 2
    mean = jnp.concatenate([total[:, :half], total[:, half:]], axis=0)
    mean_ref[...] = mean
    rank = mean.shape[0]
    peers = rank * GROUPS
    length = msg_ref.shape[0] // peers
    width = c_ref.shape[1] // GROUPS
    tiles = width // LANES
    for j in range(GROUPS):
        cols = slice(j * width, (j + 1) * width)
        local = g_ref[0, :, cols] + f_ref[0, :, cols]
        c_ref[:, cols] = local
        out = dot(mean, local, 1, 0)
        for i in range(tiles):
            msg_ref[pl.ds(j * length + i, rank, stride=GROUPS * length), :] = out[:, i * LANES : (i + 1) * LANES]
    tiled = jnp.concatenate([mean] * (LANES // rank), axis=0)
    gram = dot(mean, tiled, 1, 1)
    share = rank // replicas
    row = lax.broadcasted_iota(jnp.int32, (rank, LANES), 0)
    lane = lax.broadcasted_iota(jnp.int32, (rank, LANES), 1)
    mine = row - share * lax.axis_index("dp")
    kept = (lane >= rank * mine) & (lane < rank * (mine + 1)) & (mine >= 0) & (mine < share)
    line = jnp.sum(jnp.where(kept, gram, 0.0), axis=0, keepdims=True)
    msg_ref[pl.ds(tiles, peers, stride=length), :] = jnp.broadcast_to(line, (peers, LANES))


def sum_kernel(replicas, in_ref, out_ref, gram_ref, part):
    peers = in_ref.shape[0] // 6
    total = in_ref[0:24]
    for s in range(1, peers // 4):
        total = total + in_ref[24 * s : 24 * (s + 1)]
    part[...] = total
    for i in range(5):
        line = jnp.sum(part[pl.ds(i, 4, stride=6), :], axis=0, keepdims=True)
        out_ref[pl.ds(i, peers, stride=5), :] = jnp.broadcast_to(line, (peers, LANES))
    shards = peers // replicas
    for n in range(replicas):
        terms = in_ref[pl.ds(n * shards * 6 + 5, shards, stride=6), :]
        line = jnp.sum(terms, axis=0, keepdims=True)
        share = gram_ref.shape[0] // replicas
        gram_ref[n * share : (n + 1) * share, :] = jnp.broadcast_to(line, (share, LANES))


def inverse_factor(spread, replicas):
    rank = spread.shape[0]
    share = rank // replicas
    row = lax.broadcasted_iota(jnp.int32, (rank, LANES), 0)
    lane = lax.broadcasted_iota(jnp.int32, (rank, LANES), 1)
    at = lane - rank * (row % share)
    cols = [
        jnp.broadcast_to(jnp.sum(jnp.where(at == j, spread, 0.0), axis=1, keepdims=True), (rank, LANES))
        for j in range(rank)
    ]
    right = jnp.where(row == lane, 1.0, 0.0)
    pivots = jnp.ones((rank, LANES), jnp.float32)
    for k in range(rank):
        pivot = cols[k][k : k + 1]
        pivots = jnp.where(row == k, pivot, pivots)
        factor = jnp.where(row > k, cols[k] * (1.0 / pivot), 0.0)
        for j in range(k + 1, rank):
            cols[j] = cols[j] - factor * cols[j][k : k + 1]
        right = right - factor * right[k : k + 1]
    return right * (1.0 / jnp.sqrt(pivots))


def finish_kernel(replicas, gram_ref, all_ref, mean_ref, c_ref, nf_hbm, po_ref, qf_hbm, nf_buf, qf_buf, sems):
    rank = mean_ref.shape[0]
    whole = inverse_factor(gram_ref[...], replicas)
    lower = whole[:, :rank]
    left = dot(lower, mean_ref[...], 1, 0)
    po_ref[...] = left
    scaled = lower * (1.0 / replicas)
    width = c_ref.shape[1] // GROUPS
    tiles = width // LANES
    copies = []
    for j in range(GROUPS):
        raw = jnp.concatenate(
            [all_ref[pl.ds(j * tiles + i, rank, stride=GROUPS * tiles), :] for i in range(tiles)], axis=1
        )
        factor = dot(scaled, raw, 1, 0)
        cols = slice(j * width, (j + 1) * width)
        qf_buf[:, cols] = factor
        nf_buf[:, cols] = c_ref[:, cols] - dot(left, factor, 0, 0)
        at = pl.ds(j * width, width)
        part = [
            pltpu.make_async_copy(nf_buf.at[:, at], nf_hbm.at[0, :, at], sems.at[0, j]),
            pltpu.make_async_copy(qf_buf.at[:, at], qf_hbm.at[:, at], sems.at[1, j]),
        ]
        for copy in part:
            copy.start()
        copies += part
    for copy in copies:
        copy.wait()


def body(gradient, feedback, q_previous):
    f32 = jnp.float32
    dp, mp = lax.axis_size("dp"), lax.axis_size("mp")
    _, rows, width = gradient.shape
    rank = q_previous.shape[0]
    peers = dp * mp
    tiles = width // GROUPS // LANES
    vmem = pl.BlockSpec(memory_space=pltpu.VMEM)
    hbm = pl.BlockSpec(memory_space=pltpu.HBM)
    params = pltpu.CompilerParams(vmem_limit_bytes=16 * 2**20)

    p_out = pl.pallas_call(
        correct_kernel,
        in_specs=[hbm, hbm, hbm],
        out_specs=vmem,
        out_shape=jax.ShapeDtypeStruct((dp, rank // 2, 2 * rows), f32),
        scratch_shapes=[
            pltpu.VMEM((rows, width), f32),
            pltpu.VMEM((rows, width), f32),
            pltpu.VMEM((rank, width), f32),
            pltpu.SemaphoreType.DMA((3, IN_PARTS)),
        ],
        compiler_params=pltpu.CompilerParams(vmem_limit_bytes=60 * 2**20),
        name="correct",
    )(gradient, feedback, q_previous)
    p_all = lax.all_to_all(p_out, "dp", 0, 0, tiled=True)

    msg, p_mean, local = pl.pallas_call(
        project_kernel,
        in_specs=[vmem] * 3,
        out_specs=[vmem] * 3,
        out_shape=[
            jax.ShapeDtypeStruct((peers * (tiles + 1), LANES), f32),
            jax.ShapeDtypeStruct((rank, rows), f32),
            jax.ShapeDtypeStruct((rows, width), f32),
        ],
        compiler_params=params,
        name="project",
    )(p_all, gradient, feedback)
    msg = msg.reshape(peers, 1, (tiles + 1) * LANES)
    terms = lax.all_to_all(msg, ("dp", "mp"), 0, 0, tiled=True)

    own, gram = pl.pallas_call(
        functools.partial(sum_kernel, dp),
        in_specs=[vmem],
        out_specs=[vmem, vmem],
        out_shape=[
            jax.ShapeDtypeStruct((peers * tiles, LANES), f32),
            jax.ShapeDtypeStruct((rank, LANES), f32),
        ],
        scratch_shapes=[pltpu.VMEM((24, LANES), f32)],
        compiler_params=params,
        name="sum_terms",
    )(terms.reshape(peers * (tiles + 1), LANES))
    own = own.reshape(peers, 1, tiles * LANES)
    whole = lax.all_to_all(own, ("dp", "mp"), 0, 0, tiled=True)

    new_feedback, p_ortho, q_factor = pl.pallas_call(
        functools.partial(finish_kernel, dp),
        in_specs=[vmem] * 4,
        out_specs=[hbm, vmem, hbm],
        out_shape=[
            jax.ShapeDtypeStruct((1, rows, width), f32),
            jax.ShapeDtypeStruct((rank, rows), f32),
            jax.ShapeDtypeStruct((rank, width), f32),
        ],
        scratch_shapes=[
            pltpu.VMEM((rows, width), f32),
            pltpu.VMEM((rank, width), f32),
            pltpu.SemaphoreType.DMA((2, GROUPS)),
        ],
        compiler_params=params,
        name="finish",
    )(gram, whole.reshape(peers * tiles, LANES), p_mean, local)
    return (new_feedback, p_ortho, q_factor)


def solution(mesh):
    return jax.shard_map(
        body,
        mesh=mesh,
        in_specs=(P("dp", "mp", None), P("dp", "mp", None), P()),
        out_specs=(P("dp", "mp", None), P(None, "mp"), P()),
        check_vma=False,
    )
```

```python
import functools

import jax
import jax.numpy as jnp
from jax import lax
from jax.experimental import pallas as pl
from jax.experimental.pallas import tpu as pltpu
from jax.sharding import PartitionSpec as P

LANES = 128
IN_PARTS = 5
IN_TILE = 512
GROUPS = 8


def dot(left, right, left_dim, right_dim):
    return lax.dot_general(
        left,
        right,
        (((left_dim,), (right_dim,)), ((), ())),
        precision=lax.Precision.HIGHEST,
        preferred_element_type=jnp.float32,
    )


def split(x):
    high = x.astype(jnp.bfloat16)
    rest = x - high.astype(jnp.float32)
    mid = rest.astype(jnp.bfloat16)
    low = (rest - mid.astype(jnp.float32)).astype(jnp.bfloat16)
    return high, mid, low


def bf16_dot(left, right, left_dim, right_dim):
    return lax.dot_general(
        left, right, (((left_dim,), (right_dim,)), ((), ())), preferred_element_type=jnp.float32
    )


def fold(x, size, axis):
    parts = [lax.slice_in_dim(x, n * size, (n + 1) * size, axis=axis) for n in range(3)]
    return (parts[2] + parts[1]) + parts[0]


def correct_kernel(g_hbm, f_hbm, q_hbm, p_ref, g_buf, f_buf, q_buf, sems):
    width = g_buf.shape[1] // IN_PARTS
    copies = []
    for s in range(IN_PARTS):
        cols = pl.ds(s * width, width)
        part = [
            pltpu.make_async_copy(g_hbm.at[0, :, cols], g_buf.at[:, cols], sems.at[0, s]),
            pltpu.make_async_copy(f_hbm.at[0, :, cols], f_buf.at[:, cols], sems.at[1, s]),
            pltpu.make_async_copy(q_hbm.at[:, cols], q_buf.at[:, cols], sems.at[2, s]),
        ]
        for copy in part:
            copy.start()
        copies.append(part)
    total = None
    for s in range(IN_PARTS):
        for copy in copies[s]:
            copy.wait()
        for at in range(s * width, (s + 1) * width, IN_TILE):
            cols = slice(at, at + IN_TILE)
            local = g_buf[:, cols] + f_buf[:, cols]
            left = jnp.concatenate(split(q_buf[:, cols]), axis=0)
            right = jnp.concatenate(split(local), axis=0)
            part = bf16_dot(left, right, 1, 1)
            total = part if total is None else total + part
    total = fold(fold(total, total.shape[0] // 3, 0), total.shape[1] // 3, 1)
    half = total.shape[0] // 2
    packed = jnp.concatenate([total[:half], total[half:]], axis=1)
    p_ref[...] = jnp.broadcast_to(packed[None], p_ref.shape)


def project_kernel(p_ref, g_ref, f_ref, msg_ref, mean_ref, c_ref):
    replicas = p_ref.shape[0]
    total = p_ref[0]
    for n in range(1, replicas):
        total = total + p_ref[n]
    total = total * (1.0 / replicas)
    half = total.shape[1] // 2
    mean = jnp.concatenate([total[:, :half], total[:, half:]], axis=0)
    mean_ref[...] = mean
    rank = mean.shape[0]
    peers = rank * GROUPS
    length = msg_ref.shape[0] // peers
    width = c_ref.shape[1] // GROUPS
    tiles = width // LANES
    high, mid, low = split(mean)
    none = jnp.zeros_like(high)
    left = jnp.concatenate(
        [jnp.concatenate(parts, axis=1) for parts in ((high, high, high), (mid, mid, none), (low, none, none))], axis=0
    )
    for j in range(GROUPS):
        cols = slice(j * width, (j + 1) * width)
        local = g_ref[0, :, cols] + f_ref[0, :, cols]
        c_ref[:, cols] = local
        right = jnp.concatenate(split(local), axis=0)
        out = fold(bf16_dot(left, right, 1, 0), rank, 0)
        for i in range(tiles):
            msg_ref[pl.ds(j * length + i, rank, stride=GROUPS * length), :] = out[:, i * LANES : (i + 1) * LANES]
    tiled = jnp.concatenate([mean] * (LANES // rank), axis=0)
    gram = dot(mean, tiled, 1, 1)
    share = rank // replicas
    row = lax.broadcasted_iota(jnp.int32, (rank, LANES), 0)
    lane = lax.broadcasted_iota(jnp.int32, (rank, LANES), 1)
    mine = row - share * lax.axis_index("dp")
    kept = (lane >= rank * mine) & (lane < rank * (mine + 1)) & (mine >= 0) & (mine < share)
    line = jnp.sum(jnp.where(kept, gram, 0.0), axis=0, keepdims=True)
    msg_ref[pl.ds(tiles, peers, stride=length), :] = jnp.broadcast_to(line, (peers, LANES))


def sum_kernel(replicas, in_ref, out_ref, gram_ref, part):
    peers = in_ref.shape[0] // 6
    total = in_ref[0:24]
    for s in range(1, peers // 4):
        total = total + in_ref[24 * s : 24 * (s + 1)]
    part[...] = total
    for i in range(5):
        line = jnp.sum(part[pl.ds(i, 4, stride=6), :], axis=0, keepdims=True)
        out_ref[pl.ds(i, peers, stride=5), :] = jnp.broadcast_to(line, (peers, LANES))
    shards = peers // replicas
    for n in range(replicas):
        terms = in_ref[pl.ds(n * shards * 6 + 5, shards, stride=6), :]
        line = jnp.sum(terms, axis=0, keepdims=True)
        share = gram_ref.shape[0] // replicas
        gram_ref[n * share : (n + 1) * share, :] = jnp.broadcast_to(line, (share, LANES))


def inverse_factor(spread, replicas):
    rank = spread.shape[0]
    share = rank // replicas
    row = lax.broadcasted_iota(jnp.int32, (rank, LANES), 0)
    lane = lax.broadcasted_iota(jnp.int32, (rank, LANES), 1)
    at = lane - rank * (row % share)
    cols = [
        jnp.broadcast_to(jnp.sum(jnp.where(at == j, spread, 0.0), axis=1, keepdims=True), (rank, LANES))
        for j in range(rank)
    ]
    right = jnp.where(row == lane, 1.0, 0.0)
    pivots = jnp.ones((rank, LANES), jnp.float32)
    for k in range(rank):
        pivot = cols[k][k : k + 1]
        pivots = jnp.where(row == k, pivot, pivots)
        factor = jnp.where(row > k, cols[k] * (1.0 / pivot), 0.0)
        for j in range(k + 1, rank):
            cols[j] = cols[j] - factor * cols[j][k : k + 1]
        right = right - factor * right[k : k + 1]
    return right * (1.0 / jnp.sqrt(pivots))


def finish_kernel(
    replicas, gram_ref, all_ref, mean_ref, c_ref, nf_hbm, po_hbm, qf_hbm, nf_buf, po_buf, qf_buf, sems, po_sem
):
    rank = mean_ref.shape[0]
    whole = inverse_factor(gram_ref[...], replicas)
    lower = whole[:, :rank]
    ortho = dot(lower, mean_ref[...], 1, 0)
    po_buf[...] = ortho
    copies = [pltpu.make_async_copy(po_buf, po_hbm, po_sem)]
    copies[0].start()
    scaled = lower * (1.0 / replicas)
    both = jnp.concatenate([scaled, dot(ortho, scaled, 0, 0)], axis=0)
    high, mid, low = split(both)
    left = jnp.concatenate([high, high, mid, high, low, mid], axis=1)
    width = c_ref.shape[1] // GROUPS
    tiles = width // LANES
    for j in range(GROUPS):
        raw = jnp.concatenate(
            [all_ref[pl.ds(j * tiles + i, rank, stride=GROUPS * tiles), :] for i in range(tiles)], axis=1
        )
        high, mid, low = split(raw)
        out = bf16_dot(left, jnp.concatenate([high, mid, high, low, high, mid], axis=0), 1, 0)
        cols = slice(j * width, (j + 1) * width)
        qf_buf[:, cols] = out[:rank]
        nf_buf[:, cols] = c_ref[:, cols] - out[rank:]
        at = pl.ds(j * width, width)
        part = [
            pltpu.make_async_copy(nf_buf.at[:, at], nf_hbm.at[0, :, at], sems.at[0, j]),
            pltpu.make_async_copy(qf_buf.at[:, at], qf_hbm.at[:, at], sems.at[1, j]),
        ]
        for copy in part:
            copy.start()
        copies += part
    for copy in copies:
        copy.wait()


def body(gradient, feedback, q_previous):
    f32 = jnp.float32
    dp, mp = lax.axis_size("dp"), lax.axis_size("mp")
    _, rows, width = gradient.shape
    rank = q_previous.shape[0]
    peers = dp * mp
    tiles = width // GROUPS // LANES
    vmem = pl.BlockSpec(memory_space=pltpu.VMEM)
    hbm = pl.BlockSpec(memory_space=pltpu.HBM)
    params = pltpu.CompilerParams(vmem_limit_bytes=16 * 2**20)

    p_out = pl.pallas_call(
        correct_kernel,
        in_specs=[hbm, hbm, hbm],
        out_specs=vmem,
        out_shape=jax.ShapeDtypeStruct((dp, rank // 2, 2 * rows), f32),
        scratch_shapes=[
            pltpu.VMEM((rows, width), f32),
            pltpu.VMEM((rows, width), f32),
            pltpu.VMEM((rank, width), f32),
            pltpu.SemaphoreType.DMA((3, IN_PARTS)),
        ],
        compiler_params=pltpu.CompilerParams(vmem_limit_bytes=int(53.75 * 2**20)),
        name="correct",
    )(gradient, feedback, q_previous)
    p_all = lax.all_to_all(p_out, "dp", 0, 0, tiled=True)

    msg, p_mean, local = pl.pallas_call(
        project_kernel,
        in_specs=[vmem] * 3,
        out_specs=[vmem] * 3,
        out_shape=[
            jax.ShapeDtypeStruct((peers * (tiles + 1), LANES), f32),
            jax.ShapeDtypeStruct((rank, rows), f32),
            jax.ShapeDtypeStruct((rows, width), f32),
        ],
        compiler_params=params,
        name="project",
    )(p_all, gradient, feedback)
    msg = msg.reshape(peers, 1, (tiles + 1) * LANES)
    terms = lax.all_to_all(msg, ("dp", "mp"), 0, 0, tiled=True)

    own, gram = pl.pallas_call(
        functools.partial(sum_kernel, dp),
        in_specs=[vmem],
        out_specs=[vmem, vmem],
        out_shape=[
            jax.ShapeDtypeStruct((peers * tiles, LANES), f32),
            jax.ShapeDtypeStruct((rank, LANES), f32),
        ],
        scratch_shapes=[pltpu.VMEM((24, LANES), f32)],
        compiler_params=params,
        name="sum_terms",
    )(terms.reshape(peers * (tiles + 1), LANES))
    own = own.reshape(peers, 1, tiles * LANES)
    whole = lax.all_to_all(own, ("dp", "mp"), 0, 0, tiled=True)

    new_feedback, p_ortho, q_factor = pl.pallas_call(
        functools.partial(finish_kernel, dp),
        in_specs=[vmem] * 4,
        out_specs=[hbm] * 3,
        out_shape=[
            jax.ShapeDtypeStruct((1, rows, width), f32),
            jax.ShapeDtypeStruct((rank, rows), f32),
            jax.ShapeDtypeStruct((rank, width), f32),
        ],
        scratch_shapes=[
            pltpu.VMEM((rows, width), f32),
            pltpu.VMEM((rank, rows), f32),
            pltpu.VMEM((rank, width), f32),
            pltpu.SemaphoreType.DMA((2, GROUPS)),
            pltpu.SemaphoreType.DMA,
        ],
        compiler_params=params,
        name="finish",
    )(gram, whole.reshape(peers * tiles, LANES), p_mean, local)
    return (new_feedback, p_ortho, q_factor)


def solution(mesh):
    return jax.shard_map(
        body,
        mesh=mesh,
        in_specs=(P("dp", "mp", None), P("dp", "mp", None), P()),
        out_specs=(P("dp", "mp", None), P(None, "mp"), P()),
        check_vma=False,
    )
```

```python
import functools
import math

import jax
import jax.numpy as jnp
from jax import lax
from jax.experimental import pallas as pl
from jax.experimental.pallas import tpu as pltpu
from jax.sharding import PartitionSpec as P

LANES = 128
IN_PARTS = 5
IN_TILE = 512
GROUPS = 8
CORES = 2
DP = ("x", "core")
MP = ("z", "y")


def dot(left, right, left_dim, right_dim):
    return lax.dot_general(
        left,
        right,
        (((left_dim,), (right_dim,)), ((), ())),
        precision=lax.Precision.HIGHEST,
        preferred_element_type=jnp.float32,
    )


def split(x):
    high = x.astype(jnp.bfloat16)
    rest = x - high.astype(jnp.float32)
    mid = rest.astype(jnp.bfloat16)
    low = (rest - mid.astype(jnp.float32)).astype(jnp.bfloat16)
    return high, mid, low


def bf16_dot(left, right, left_dim, right_dim):
    return lax.dot_general(
        left, right, (((left_dim,), (right_dim,)), ((), ())), preferred_element_type=jnp.float32
    )


def fold(x, size, axis):
    parts = [lax.slice_in_dim(x, n * size, (n + 1) * size, axis=axis) for n in range(3)]
    return (parts[2] + parts[1]) + parts[0]


def correct_kernel(g_hbm, f_hbm, q_hbm, p_ref, g_buf, f_buf, q_buf, sems):
    width = g_buf.shape[1] // IN_PARTS
    copies = []
    for s in range(IN_PARTS):
        cols = pl.ds(s * width, width)
        part = [
            pltpu.make_async_copy(g_hbm.at[0, :, cols], g_buf.at[:, cols], sems.at[0, s]),
            pltpu.make_async_copy(f_hbm.at[0, :, cols], f_buf.at[:, cols], sems.at[1, s]),
            pltpu.make_async_copy(q_hbm.at[:, cols], q_buf.at[:, cols], sems.at[2, s]),
        ]
        for copy in part:
            copy.start()
        copies.append(part)
    total = None
    for s in range(IN_PARTS):
        for copy in copies[s]:
            copy.wait()
        for at in range(s * width, (s + 1) * width, IN_TILE):
            cols = slice(at, at + IN_TILE)
            local = g_buf[:, cols] + f_buf[:, cols]
            left = jnp.concatenate(split(q_buf[:, cols]), axis=0)
            right = jnp.concatenate(split(local), axis=0)
            part = bf16_dot(left, right, 1, 1)
            total = part if total is None else total + part
    total = fold(fold(total, total.shape[0] // 3, 0), total.shape[1] // 3, 1)
    half = total.shape[0] // 2
    packed = jnp.concatenate([total[:half], total[half:]], axis=1)
    p_ref[...] = jnp.broadcast_to(packed[None], p_ref.shape)


def owner_of(group):
    return group % (GROUPS // CORES) * CORES + group // (GROUPS // CORES)


def project_kernel(p_ref, g_ref, f_ref, msg_ref, mean_ref, c_ref):
    replicas = p_ref.shape[0]
    total = p_ref[0]
    for n in range(1, replicas):
        total = total + p_ref[n]
    total = total * (1.0 / replicas)
    half = total.shape[1] // 2
    mean = jnp.concatenate([total[:, :half], total[:, half:]], axis=0)
    mean_ref[...] = mean
    rank = mean.shape[0]
    peers = rank * GROUPS
    length = msg_ref.shape[0] // peers
    width = c_ref.shape[1] // GROUPS
    tiles = width // LANES
    high, mid, low = split(mean)
    none = jnp.zeros_like(high)
    left = jnp.concatenate(
        [jnp.concatenate(parts, axis=1) for parts in ((high, high, high), (mid, mid, none), (low, none, none))], axis=0
    )
    for j in range(GROUPS):
        cols = slice(j * width, (j + 1) * width)
        local = g_ref[0, :, cols] + f_ref[0, :, cols]
        c_ref[:, cols] = local
        right = jnp.concatenate(split(local), axis=0)
        out = fold(bf16_dot(left, right, 1, 0), rank, 0)
        for i in range(tiles):
            first = owner_of(j) * rank * length + i
            msg_ref[pl.ds(first, rank, stride=length), :] = out[:, i * LANES : (i + 1) * LANES]
    tiled = jnp.concatenate([mean] * (LANES // rank), axis=0)
    gram = dot(mean, tiled, 1, 1)
    share = rank // replicas
    row = lax.broadcasted_iota(jnp.int32, (rank, LANES), 0)
    lane = lax.broadcasted_iota(jnp.int32, (rank, LANES), 1)
    mine = row - share * lax.axis_index(DP)
    kept = (lane >= rank * mine) & (lane < rank * (mine + 1)) & (mine >= 0) & (mine < share)
    line = jnp.sum(jnp.where(kept, gram, 0.0), axis=0, keepdims=True)
    msg_ref[pl.ds(tiles, peers, stride=length), :] = jnp.broadcast_to(line, (peers, LANES))


def sum_kernel(replicas, in_ref, out_ref, gram_ref, part):
    peers = in_ref.shape[0] // 6
    total = in_ref[0:24]
    for s in range(1, peers // 4):
        total = total + in_ref[24 * s : 24 * (s + 1)]
    part[...] = total
    for i in range(5):
        line = jnp.sum(part[pl.ds(i, 4, stride=6), :], axis=0, keepdims=True)
        copies = out_ref.shape[0] // 5
        out_ref[pl.ds(i, copies, stride=5), :] = jnp.broadcast_to(line, (copies, LANES))
    shards = peers // replicas
    for n in range(replicas):
        terms = in_ref[pl.ds(n * shards * 6 + 5, shards, stride=6), :]
        line = jnp.sum(terms, axis=0, keepdims=True)
        share = gram_ref.shape[0] // replicas
        gram_ref[n * share : (n + 1) * share, :] = jnp.broadcast_to(line, (share, LANES))


def inverse_factor(spread, replicas):
    rank = spread.shape[0]
    share = rank // replicas
    row = lax.broadcasted_iota(jnp.int32, (rank, LANES), 0)
    lane = lax.broadcasted_iota(jnp.int32, (rank, LANES), 1)
    at = lane - rank * (row % share)
    cols = [
        jnp.broadcast_to(jnp.sum(jnp.where(at == j, spread, 0.0), axis=1, keepdims=True), (rank, LANES))
        for j in range(rank)
    ]
    right = jnp.where(row == lane, 1.0, 0.0)
    pivots = jnp.ones((rank, LANES), jnp.float32)
    for k in range(rank):
        pivot = cols[k][k : k + 1]
        pivots = jnp.where(row == k, pivot, pivots)
        factor = jnp.where(row > k, cols[k] * (1.0 / pivot), 0.0)
        for j in range(k + 1, rank):
            cols[j] = cols[j] - factor * cols[j][k : k + 1]
        right = right - factor * right[k : k + 1]
    return right * (1.0 / jnp.sqrt(pivots))


def half_block(left, half_ref, c_ref, core, n, rank):
    groups = GROUPS // CORES
    width = c_ref.shape[1] // GROUPS
    tiles = width // LANES
    raw = jnp.concatenate(
        [half_ref[pl.ds(n * rank * tiles + i, rank, stride=tiles), :] for i in range(tiles)], axis=1
    )
    high, mid, low = split(raw)
    out = bf16_dot(left, jnp.concatenate([high, mid, high, low, high, mid], axis=0), 1, 0)
    at = pl.multiple_of((core * groups + n) * width, width)
    return out[:rank], c_ref[:, pl.ds(at, width)] - out[rank:]


def own_half_kernel(replicas, gram_ref, half_ref, mean_ref, c_ref, left_ref, po_ref, qf_ref, nf_ref):
    rank = mean_ref.shape[0]
    whole = inverse_factor(gram_ref[...], replicas)
    lower = whole[:, :rank]
    ortho = dot(lower, mean_ref[...], 1, 0)
    po_ref[...] = ortho
    scaled = lower * (1.0 / replicas)
    both = jnp.concatenate([scaled, dot(ortho, scaled, 0, 0)], axis=0)
    high, mid, low = split(both)
    left = jnp.concatenate([high, high, mid, high, low, mid], axis=1)
    left_ref[...] = left
    width = c_ref.shape[1] // GROUPS
    for n in range(GROUPS // CORES):
        cols = slice(n * width, (n + 1) * width)
        qf_ref[:, cols], nf_ref[:, cols] = half_block(left, half_ref, c_ref, lax.axis_index("core"), n, rank)


def finish_kernel(
    left_ref, po_ref, qf_ref, nf_ref, half_ref, c_ref, nf_hbm, po_hbm, qf_hbm, nf_buf, qf_buf, sems, half_sems
):
    rank = po_ref.shape[0]
    core = lax.axis_index("core")
    width = c_ref.shape[1] // GROUPS
    groups = GROUPS // CORES
    own = pl.ds(pl.multiple_of(core * groups * width, width), groups * width)
    copies = [
        pltpu.make_async_copy(nf_ref, nf_hbm.at[0, :, own], half_sems.at[0]),
        pltpu.make_async_copy(qf_ref, qf_hbm.at[:, own], half_sems.at[1]),
        pltpu.make_async_copy(po_ref, po_hbm, half_sems.at[2]),
    ]
    for copy in copies:
        copy.start()
    left = left_ref[...]
    for n in range(groups):
        cols = slice(n * width, (n + 1) * width)
        qf_buf[:, cols], nf_buf[:, cols] = half_block(left, half_ref, c_ref, 1 - core, n, rank)
        here = pl.ds(n * width, width)
        there = pl.ds(pl.multiple_of(((1 - core) * groups + n) * width, width), width)
        part = [
            pltpu.make_async_copy(nf_buf.at[:, here], nf_hbm.at[0, :, there], sems.at[0, n]),
            pltpu.make_async_copy(qf_buf.at[:, here], qf_hbm.at[:, there], sems.at[1, n]),
        ]
        for copy in part:
            copy.start()
        copies += part
    for copy in copies:
        copy.wait()


def body(gradient, feedback, q_previous):
    f32 = jnp.float32
    dp, mp = lax.axis_size(DP), lax.axis_size(MP)
    _, rows, width = gradient.shape
    rank = q_previous.shape[0]
    peers = dp * mp
    tiles = width // GROUPS // LANES
    vmem = pl.BlockSpec(memory_space=pltpu.VMEM)
    hbm = pl.BlockSpec(memory_space=pltpu.HBM)
    params = pltpu.CompilerParams(vmem_limit_bytes=16 * 2**20)

    p_out = pl.pallas_call(
        correct_kernel,
        in_specs=[hbm, hbm, hbm],
        out_specs=vmem,
        out_shape=jax.ShapeDtypeStruct((dp, rank // 2, 2 * rows), f32),
        scratch_shapes=[
            pltpu.VMEM((rows, width), f32),
            pltpu.VMEM((rows, width), f32),
            pltpu.VMEM((rank, width), f32),
            pltpu.SemaphoreType.DMA((3, IN_PARTS)),
        ],
        compiler_params=pltpu.CompilerParams(vmem_limit_bytes=int(53.75 * 2**20)),
        name="correct",
    )(gradient, feedback, q_previous)
    p_all = lax.all_to_all(p_out, DP, 0, 0, tiled=True)

    msg, p_mean, local = pl.pallas_call(
        project_kernel,
        in_specs=[vmem] * 3,
        out_specs=[vmem] * 3,
        out_shape=[
            jax.ShapeDtypeStruct((peers * (tiles + 1), LANES), f32),
            jax.ShapeDtypeStruct((rank, rows), f32),
            jax.ShapeDtypeStruct((rows, width), f32),
        ],
        compiler_params=params,
        name="project",
    )(p_all, gradient, feedback)
    msg = msg.reshape(peers, 1, (tiles + 1) * LANES)
    terms = lax.all_to_all(msg, DP + MP, 0, 0, tiled=True)

    own, gram = pl.pallas_call(
        functools.partial(sum_kernel, dp),
        in_specs=[vmem],
        out_specs=[vmem, vmem],
        out_shape=[
            jax.ShapeDtypeStruct((peers // CORES * tiles, LANES), f32),
            jax.ShapeDtypeStruct((rank, LANES), f32),
        ],
        scratch_shapes=[pltpu.VMEM((24, LANES), f32)],
        compiler_params=params,
        name="sum_terms",
    )(terms.reshape(peers * (tiles + 1), LANES))
    own = own.reshape(peers // CORES, 1, tiles * LANES)
    half = lax.all_to_all(own, ("x",) + MP, 0, 0, tiled=True).reshape(peers // CORES * tiles, LANES)
    other = lax.ppermute(half, "core", [(0, 1), (1, 0)])

    left, p_ortho, q_half, f_half = pl.pallas_call(
        functools.partial(own_half_kernel, dp),
        in_specs=[vmem] * 4,
        out_specs=[vmem] * 4,
        out_shape=[
            jax.ShapeDtypeStruct((rank + rows, 6 * rank), jnp.bfloat16),
            jax.ShapeDtypeStruct((rank, rows), f32),
            jax.ShapeDtypeStruct((rank, width // CORES), f32),
            jax.ShapeDtypeStruct((rows, width // CORES), f32),
        ],
        compiler_params=params,
        cost_estimate=pl.CostEstimate(flops=2 * rows * width * 96, bytes_accessed=8 * rows * width, transcendentals=0),
        name="own_half",
    )(gram, half, p_mean, local)
    new_feedback, p_ortho, q_factor = pl.pallas_call(
        finish_kernel,
        in_specs=[vmem] * 6,
        out_specs=[hbm] * 3,
        out_shape=[
            jax.ShapeDtypeStruct((1, rows, width), f32),
            jax.ShapeDtypeStruct((rank, rows), f32),
            jax.ShapeDtypeStruct((rank, width), f32),
        ],
        scratch_shapes=[
            pltpu.VMEM((rows, width // CORES), f32),
            pltpu.VMEM((rank, width // CORES), f32),
            pltpu.SemaphoreType.DMA((2, GROUPS // CORES)),
            pltpu.SemaphoreType.DMA((3,)),
        ],
        compiler_params=params,
        name="finish",
    )(left, p_ortho, q_half, f_half, other, local)
    return (new_feedback, p_ortho, q_factor)


def solution(mesh):
    sizes = (mesh.shape["dp"] // CORES, CORES, math.isqrt(mesh.shape["mp"]), math.isqrt(mesh.shape["mp"]))
    fine = jax.sharding.Mesh(mesh.devices.reshape(sizes), DP + MP)
    return jax.shard_map(
        body,
        mesh=fine,
        in_specs=(P(DP, MP, None), P(DP, MP, None), P()),
        out_specs=(P(DP, MP, None), P(None, MP), P()),
        check_vma=False,
    )
```

```python
import functools
import math

import jax
import jax.numpy as jnp
from jax import lax
from jax.experimental import pallas as pl
from jax.experimental.pallas import tpu as pltpu
from jax.sharding import PartitionSpec as P

LANES = 128
IN_PARTS = 5
IN_TILE = 512
CORES = 2
HALF_GROUPS = 4
DP = ("x", "core")
MP = ("z", "y")


def dot(left, right, left_dim, right_dim):
    return lax.dot_general(
        left,
        right,
        (((left_dim,), (right_dim,)), ((), ())),
        precision=lax.Precision.HIGHEST,
        preferred_element_type=jnp.float32,
    )


def split(x):
    high = x.astype(jnp.bfloat16)
    rest = x - high.astype(jnp.float32)
    mid = rest.astype(jnp.bfloat16)
    low = (rest - mid.astype(jnp.float32)).astype(jnp.bfloat16)
    return high, mid, low


def bf16_dot(left, right, left_dim, right_dim):
    return lax.dot_general(
        left, right, (((left_dim,), (right_dim,)), ((), ())), preferred_element_type=jnp.float32
    )


def fold(x, size, axis):
    parts = [lax.slice_in_dim(x, n * size, (n + 1) * size, axis=axis) for n in range(3)]
    return (parts[2] + parts[1]) + parts[0]


def correct_kernel(g_hbm, f_hbm, q_hbm, p_ref, g_buf, f_buf, q_buf, sems):
    width = g_buf.shape[1] // IN_PARTS
    copies = []
    for s in range(IN_PARTS):
        cols = pl.ds(s * width, width)
        part = [
            pltpu.make_async_copy(g_hbm.at[0, :, cols], g_buf.at[:, cols], sems.at[0, s]),
            pltpu.make_async_copy(f_hbm.at[0, :, cols], f_buf.at[:, cols], sems.at[1, s]),
            pltpu.make_async_copy(q_hbm.at[:, cols], q_buf.at[:, cols], sems.at[2, s]),
        ]
        for copy in part:
            copy.start()
        copies.append(part)
    total = None
    for s in range(IN_PARTS):
        for copy in copies[s]:
            copy.wait()
        for at in range(s * width, (s + 1) * width, IN_TILE):
            cols = slice(at, at + IN_TILE)
            local = g_buf[:, cols] + f_buf[:, cols]
            left = jnp.concatenate(split(q_buf[:, cols]), axis=0)
            right = jnp.concatenate(split(local), axis=0)
            part = bf16_dot(left, right, 1, 1)
            total = part if total is None else total + part
    total = fold(fold(total, total.shape[0] // 3, 0), total.shape[1] // 3, 1)
    half = total.shape[0] // 2
    packed = jnp.concatenate([total[:half], total[half:]], axis=1)
    p_ref[...] = jnp.broadcast_to(packed[None], p_ref.shape)


def member_of(place):
    return (6 - place) % 4


def chip_groups(sizes):
    nx, nc, nz, ny = sizes
    return [
        [
            ((member_of(i) * nc + core) * nz + member_of(j)) * ny + member_of(k)
            for i in range(nx)
            for j in range(nz)
            for k in range(ny)
        ]
        for core in range(nc)
    ]


def column_at(core, n, width):
    return pl.multiple_of((core * HALF_GROUPS + n) * width, width)


def write_half(mean, core, g_ref, f_ref, msg_ref, c_ref):
    rank = mean.shape[0]
    width = c_ref.shape[1] // HALF_GROUPS
    tiles = width // LANES
    high, mid, low = split(mean)
    none = jnp.zeros_like(high)
    left = jnp.concatenate(
        [jnp.concatenate(parts, axis=1) for parts in ((high, high, high), (mid, mid, none), (low, none, none))], axis=0
    )
    for n in range(HALF_GROUPS):
        cols = pl.ds(column_at(core, n, width), width)
        local = g_ref[0, :, cols] + f_ref[0, :, cols]
        c_ref[:, n * width : (n + 1) * width] = local
        out = fold(bf16_dot(left, jnp.concatenate(split(local), axis=0), 1, 0), rank, 0)
        for i in range(tiles):
            first = n * rank * (tiles + 1) + i
            msg_ref[pl.ds(first, rank, stride=tiles + 1), :] = out[:, i * LANES : (i + 1) * LANES]


def write_last(msg_ref, line):
    count = msg_ref.shape[0] // 6
    msg_ref[pl.ds(5, count, stride=6), :] = jnp.broadcast_to(line, (count, LANES))


def other_kernel(p_ref, g_ref, f_ref, msg_ref, mean_ref, c_ref):
    replicas = p_ref.shape[0]
    total = p_ref[0]
    for n in range(1, replicas):
        total = total + p_ref[n]
    total = total * (1.0 / replicas)
    half = total.shape[1] // 2
    mean = jnp.concatenate([total[:, :half], total[:, half:]], axis=0)
    mean_ref[...] = mean
    write_half(mean, 1 - lax.axis_index("core"), g_ref, f_ref, msg_ref, c_ref)
    write_last(msg_ref, jnp.zeros((1, LANES), jnp.float32))


def own_kernel(mean_ref, g_ref, f_ref, msg_ref, c_ref):
    mean = mean_ref[...]
    rank = mean.shape[0]
    write_half(mean, lax.axis_index("core"), g_ref, f_ref, msg_ref, c_ref)
    gram = dot(mean, jnp.concatenate([mean] * (LANES // rank), axis=0), 1, 1)
    share = rank // HALF_GROUPS
    row = lax.broadcasted_iota(jnp.int32, (rank, LANES), 0)
    lane = lax.broadcasted_iota(jnp.int32, (rank, LANES), 1)
    mine = row - share * member_of(lax.axis_index("x"))
    kept = (lane >= rank * mine) & (lane < rank * (mine + 1)) & (mine >= 0) & (mine < share)
    write_last(msg_ref, jnp.sum(jnp.where(kept, gram, 0.0), axis=0, keepdims=True))


def sum_kernel(in_ref, out_ref, gram_ref, part):
    peers = in_ref.shape[0] // 6
    total = in_ref[0:24]
    for s in range(1, peers // 4):
        total = total + in_ref[24 * s : 24 * (s + 1)]
    part[...] = total
    for i in range(5):
        line = jnp.sum(part[pl.ds(i, 4, stride=6), :], axis=0, keepdims=True)
        out_ref[pl.ds(i, peers, stride=5), :] = jnp.broadcast_to(line, (peers, LANES))
    shards = peers // HALF_GROUPS
    share = gram_ref.shape[0] // HALF_GROUPS
    for n in range(HALF_GROUPS):
        terms = in_ref[pl.ds(n * shards * 6 + 5, shards, stride=6), :]
        line = jnp.sum(terms, axis=0, keepdims=True)
        gram_ref[n * share : (n + 1) * share, :] = jnp.broadcast_to(line, (share, LANES))


def inverse_factor(spread):
    rank = spread.shape[0]
    share = rank // HALF_GROUPS
    row = lax.broadcasted_iota(jnp.int32, (rank, LANES), 0)
    lane = lax.broadcasted_iota(jnp.int32, (rank, LANES), 1)
    at = lane - rank * (row % share)
    cols = [
        jnp.broadcast_to(jnp.sum(jnp.where(at == j, spread, 0.0), axis=1, keepdims=True), (rank, LANES))
        for j in range(rank)
    ]
    right = jnp.where(row == lane, 1.0, 0.0)
    pivots = jnp.ones((rank, LANES), jnp.float32)
    for k in range(rank):
        pivot = cols[k][k : k + 1]
        pivots = jnp.where(row == k, pivot, pivots)
        factor = jnp.where(row > k, cols[k] * (1.0 / pivot), 0.0)
        for j in range(k + 1, rank):
            cols[j] = cols[j] - factor * cols[j][k : k + 1]
        right = right - factor * right[k : k + 1]
    return right * (1.0 / jnp.sqrt(pivots))


def half_block(left, half_ref, c_ref, n, rank):
    width = c_ref.shape[1] // HALF_GROUPS
    tiles = width // LANES
    raw = jnp.concatenate(
        [half_ref[pl.ds(n * rank * tiles + i, rank, stride=tiles), :] for i in range(tiles)], axis=1
    )
    high, mid, low = split(raw)
    out = bf16_dot(left, jnp.concatenate([high, mid, high, low, high, mid], axis=0), 1, 0)
    return out[:rank], c_ref[:, n * width : (n + 1) * width] - out[rank:]


def own_half_kernel(replicas, gram_ref, half_ref, mean_ref, c_ref, left_ref, po_ref, qf_ref, nf_ref):
    rank = mean_ref.shape[0]
    whole = inverse_factor(gram_ref[...])
    lower = whole[:, :rank]
    ortho = dot(lower, mean_ref[...], 1, 0)
    po_ref[...] = ortho
    scaled = lower * (1.0 / replicas)
    both = jnp.concatenate([scaled, dot(ortho, scaled, 0, 0)], axis=0)
    high, mid, low = split(both)
    left = jnp.concatenate([high, high, mid, high, low, mid], axis=1)
    left_ref[...] = left
    width = c_ref.shape[1] // HALF_GROUPS
    for n in range(HALF_GROUPS):
        cols = slice(n * width, (n + 1) * width)
        qf_ref[:, cols], nf_ref[:, cols] = half_block(left, half_ref, c_ref, n, rank)


def finish_kernel(
    left_ref, po_ref, qf_ref, nf_ref, half_ref, c_ref, nf_hbm, po_hbm, qf_hbm, nf_buf, qf_buf, sems, half_sems
):
    rank = po_ref.shape[0]
    core = lax.axis_index("core")
    width = c_ref.shape[1] // HALF_GROUPS
    own = pl.ds(column_at(core, 0, width), HALF_GROUPS * width)
    copies = [
        pltpu.make_async_copy(nf_ref, nf_hbm.at[0, :, own], half_sems.at[0]),
        pltpu.make_async_copy(qf_ref, qf_hbm.at[:, own], half_sems.at[1]),
        pltpu.make_async_copy(po_ref, po_hbm, half_sems.at[2]),
    ]
    for copy in copies:
        copy.start()
    left = left_ref[...]
    for n in range(HALF_GROUPS):
        cols = slice(n * width, (n + 1) * width)
        qf_buf[:, cols], nf_buf[:, cols] = half_block(left, half_ref, c_ref, n, rank)
        here = pl.ds(n * width, width)
        there = pl.ds(column_at(1 - core, n, width), width)
        part = [
            pltpu.make_async_copy(nf_buf.at[:, here], nf_hbm.at[0, :, there], sems.at[0, n]),
            pltpu.make_async_copy(qf_buf.at[:, here], qf_hbm.at[:, there], sems.at[1, n]),
        ]
        for copy in part:
            copy.start()
        copies += part
    for copy in copies:
        copy.wait()


def body(gradient, feedback, q_previous):
    f32 = jnp.float32
    dp, mp = lax.axis_size(DP), lax.axis_size(MP)
    _, rows, width = gradient.shape
    rank = q_previous.shape[0]
    tiles = width // CORES // HALF_GROUPS // LANES
    vmem = pl.BlockSpec(memory_space=pltpu.VMEM)
    hbm = pl.BlockSpec(memory_space=pltpu.HBM)
    params = pltpu.CompilerParams(vmem_limit_bytes=16 * 2**20)

    p_out = pl.pallas_call(
        correct_kernel,
        in_specs=[hbm, hbm, hbm],
        out_specs=vmem,
        out_shape=jax.ShapeDtypeStruct((dp, rank // 2, 2 * rows), f32),
        scratch_shapes=[
            pltpu.VMEM((rows, width), f32),
            pltpu.VMEM((rows, width), f32),
            pltpu.VMEM((rank, width), f32),
            pltpu.SemaphoreType.DMA((3, IN_PARTS)),
        ],
        compiler_params=pltpu.CompilerParams(vmem_limit_bytes=int(53.75 * 2**20)),
        name="correct",
    )(gradient, feedback, q_previous)
    sizes = tuple(lax.axis_size(name) for name in DP + MP)
    near = [[member_of(i) * CORES + core for i in range(sizes[0]) for core in (1, 0)]]
    chips = chip_groups(sizes)
    p_all = lax.all_to_all(p_out, DP, 0, 0, tiled=True, axis_index_groups=near)

    count = sizes[0] * mp
    half_out = [
        jax.ShapeDtypeStruct((count * (tiles + 1), LANES), f32),
        jax.ShapeDtypeStruct((rows, width // CORES), f32),
    ]
    msg_other, p_mean, local_other = pl.pallas_call(
        other_kernel,
        in_specs=[vmem] * 3,
        out_specs=[vmem] * 3,
        out_shape=[half_out[0], jax.ShapeDtypeStruct((rank, rows), f32), half_out[1]],
        compiler_params=params,
        name="project_other",
    )(p_all, gradient, feedback)
    arrived = lax.ppermute(msg_other, "core", [(0, 1), (1, 0)])
    msg_own, local_own = pl.pallas_call(
        own_kernel,
        in_specs=[vmem] * 3,
        out_specs=[vmem] * 2,
        out_shape=half_out,
        compiler_params=params,
        cost_estimate=pl.CostEstimate(flops=2 * rows * width * 96, bytes_accessed=8 * rows * width, transcendentals=0),
        name="project_own",
    )(p_mean, gradient, feedback)
    msg = (msg_own + arrived).reshape(count, 1, (tiles + 1) * LANES)
    terms = lax.all_to_all(msg, DP + MP, 0, 0, tiled=True, axis_index_groups=chips)

    own, gram = pl.pallas_call(
        sum_kernel,
        in_specs=[vmem],
        out_specs=[vmem, vmem],
        out_shape=[
            jax.ShapeDtypeStruct((count * tiles, LANES), f32),
            jax.ShapeDtypeStruct((rank, LANES), f32),
        ],
        scratch_shapes=[pltpu.VMEM((24, LANES), f32)],
        compiler_params=params,
        name="sum_terms",
    )(terms.reshape(count * (tiles + 1), LANES))
    own = own.reshape(count, 1, tiles * LANES)
    half = lax.all_to_all(own, DP + MP, 0, 0, tiled=True, axis_index_groups=chips).reshape(count * tiles, LANES)
    other = lax.ppermute(half, "core", [(0, 1), (1, 0)])

    left, p_ortho, q_half, f_half = pl.pallas_call(
        functools.partial(own_half_kernel, dp),
        in_specs=[vmem] * 4,
        out_specs=[vmem] * 4,
        out_shape=[
            jax.ShapeDtypeStruct((rank + rows, 6 * rank), jnp.bfloat16),
            jax.ShapeDtypeStruct((rank, rows), f32),
            jax.ShapeDtypeStruct((rank, width // CORES), f32),
            jax.ShapeDtypeStruct((rows, width // CORES), f32),
        ],
        compiler_params=params,
        cost_estimate=pl.CostEstimate(flops=2 * rows * width * 96, bytes_accessed=8 * rows * width, transcendentals=0),
        name="own_half",
    )(gram, half, p_mean, local_own)
    new_feedback, p_ortho, q_factor = pl.pallas_call(
        finish_kernel,
        in_specs=[vmem] * 6,
        out_specs=[hbm] * 3,
        out_shape=[
            jax.ShapeDtypeStruct((1, rows, width), f32),
            jax.ShapeDtypeStruct((rank, rows), f32),
            jax.ShapeDtypeStruct((rank, width), f32),
        ],
        scratch_shapes=[
            pltpu.VMEM((rows, width // CORES), f32),
            pltpu.VMEM((rank, width // CORES), f32),
            pltpu.SemaphoreType.DMA((2, HALF_GROUPS)),
            pltpu.SemaphoreType.DMA((3,)),
        ],
        compiler_params=params,
        name="finish",
    )(left, p_ortho, q_half, f_half, other, local_other)
    return (new_feedback, p_ortho, q_factor)


def solution(mesh):
    sizes = (mesh.shape["dp"] // CORES, CORES, math.isqrt(mesh.shape["mp"]), math.isqrt(mesh.shape["mp"]))
    fine = jax.sharding.Mesh(mesh.devices.reshape(sizes), DP + MP)
    return jax.shard_map(
        body,
        mesh=fine,
        in_specs=(P(DP, MP, None), P(DP, MP, None), P()),
        out_specs=(P(DP, MP, None), P(None, MP), P()),
        check_vma=False,
    )
```

```python
import functools
import math

import jax
import jax.numpy as jnp
from jax import lax
from jax.experimental import pallas as pl
from jax.experimental.pallas import tpu as pltpu
from jax.sharding import PartitionSpec as P

LANES = 128
IN_PARTS = 4
IN_TILE = 640
CORES = 2
HALF_GROUPS = 4
DP = ("x", "core")
MP = ("z", "y")


def dot(left, right, left_dim, right_dim):
    return lax.dot_general(
        left,
        right,
        (((left_dim,), (right_dim,)), ((), ())),
        precision=lax.Precision.HIGHEST,
        preferred_element_type=jnp.float32,
    )


def split(x):
    high = x.astype(jnp.bfloat16)
    rest = x - high.astype(jnp.float32)
    mid = rest.astype(jnp.bfloat16)
    low = (rest - mid.astype(jnp.float32)).astype(jnp.bfloat16)
    return high, mid, low


def bf16_dot(left, right, left_dim, right_dim):
    return lax.dot_general(
        left, right, (((left_dim,), (right_dim,)), ((), ())), preferred_element_type=jnp.float32
    )


def fold(x, size, axis):
    parts = [lax.slice_in_dim(x, n * size, (n + 1) * size, axis=axis) for n in range(3)]
    return (parts[2] + parts[1]) + parts[0]


def correct_kernel(g_hbm, f_hbm, q_hbm, p_ref, c_hbm, g_buf, f_buf, q_buf, c_buf, sems, c_sems):
    half = c_buf.shape[1]
    parts = IN_PARTS // CORES
    width = half // parts
    core = lax.axis_index("core")
    copies = []
    for s in range(IN_PARTS):
        first = (1 - core if s < parts else core) * half + s % parts * width
        there = pl.ds(pl.multiple_of(first, width), width)
        here = pl.ds(s * width, width)
        part = [
            pltpu.make_async_copy(g_hbm.at[0, :, there], g_buf.at[:, here], sems.at[0, s]),
            pltpu.make_async_copy(f_hbm.at[0, :, there], f_buf.at[:, here], sems.at[1, s]),
            pltpu.make_async_copy(q_hbm.at[:, there], q_buf.at[:, here], sems.at[2, s]),
        ]
        for copy in part:
            copy.start()
        copies.append(part)
    total = None
    sends = []
    for s in range(IN_PARTS):
        for copy in copies[s]:
            copy.wait()
        for at in range(s * width, (s + 1) * width, IN_TILE):
            cols = slice(at, at + IN_TILE)
            local = g_buf[:, cols] + f_buf[:, cols]
            if s < parts:
                c_buf[:, cols] = local
            left = jnp.concatenate(split(q_buf[:, cols]), axis=0)
            right = jnp.concatenate(split(local), axis=0)
            part = bf16_dot(left, right, 1, 1)
            total = part if total is None else total + part
        if s < parts:
            cols = pl.ds(s * width, width)
            sends.append(pltpu.make_async_copy(c_buf.at[:, cols], c_hbm.at[:, cols], c_sems.at[s]))
            sends[-1].start()
    total = fold(fold(total, total.shape[0] // 3, 0), total.shape[1] // 3, 1)
    half = total.shape[0] // 2
    packed = jnp.concatenate([total[:half], total[half:]], axis=1)
    p_ref[...] = jnp.broadcast_to(packed[None], p_ref.shape)
    for copy in sends:
        copy.wait()


def member_of(place):
    return (6 - place) % 4


def chip_groups(sizes):
    nx, nc, nz, ny = sizes
    return [
        [
            ((member_of(i) * nc + core) * nz + member_of(j)) * ny + member_of(k)
            for i in range(nx)
            for j in range(nz)
            for k in range(ny)
        ]
        for core in range(nc)
    ]


def column_at(core, n, width):
    return pl.multiple_of((core * HALF_GROUPS + n) * width, width)


def project_kernel(p_ref, g_ref, f_ref, arrived_ref, msg_ref, mean_ref):
    replicas = p_ref.shape[0]
    total = p_ref[0]
    for n in range(1, replicas):
        total = total + p_ref[n]
    total = total * (1.0 / replicas)
    half = total.shape[1] // 2
    mean = jnp.concatenate([total[:, :half], total[:, half:]], axis=0)
    mean_ref[...] = mean
    rank = mean.shape[0]
    high, mid, low = split(mean)
    none = jnp.zeros_like(high)
    left = jnp.concatenate(
        [jnp.concatenate(parts, axis=1) for parts in ((high, high, high), (mid, mid, none), (low, none, none))], axis=0
    )
    width = arrived_ref.shape[1] // HALF_GROUPS
    tiles = width // LANES
    for n in range(HALF_GROUPS):
        cols = pl.ds(column_at(lax.axis_index("core"), n, width), width)
        pair = (g_ref[0, :, cols] + f_ref[0, :, cols]) + arrived_ref[:, n * width : (n + 1) * width]
        out = fold(bf16_dot(left, jnp.concatenate(split(pair), axis=0), 1, 0), rank, 0)
        for i in range(tiles):
            first = n * rank * (tiles + 1) + i
            msg_ref[pl.ds(first, rank, stride=tiles + 1), :] = out[:, i * LANES : (i + 1) * LANES]
    gram = dot(mean, jnp.concatenate([mean] * (LANES // rank), axis=0), 1, 1)
    share = rank // HALF_GROUPS
    row = lax.broadcasted_iota(jnp.int32, (rank, LANES), 0)
    lane = lax.broadcasted_iota(jnp.int32, (rank, LANES), 1)
    mine = row - share * member_of(lax.axis_index("x"))
    kept = (lane >= rank * mine) & (lane < rank * (mine + 1)) & (mine >= 0) & (mine < share)
    line = jnp.sum(jnp.where(kept, gram, 0.0), axis=0, keepdims=True)
    count = msg_ref.shape[0] // (tiles + 1)
    msg_ref[pl.ds(tiles, count, stride=tiles + 1), :] = jnp.broadcast_to(line, (count, LANES))


def sum_kernel(in_ref, out_ref, gram_ref, part):
    peers = in_ref.shape[0] // 6
    total = in_ref[0:24]
    for s in range(1, peers // 4):
        total = total + in_ref[24 * s : 24 * (s + 1)]
    part[...] = total
    for i in range(5):
        line = jnp.sum(part[pl.ds(i, 4, stride=6), :], axis=0, keepdims=True)
        out_ref[pl.ds(i, peers, stride=5), :] = jnp.broadcast_to(line, (peers, LANES))
    shards = peers // HALF_GROUPS
    share = gram_ref.shape[0] // HALF_GROUPS
    for n in range(HALF_GROUPS):
        terms = in_ref[pl.ds(n * shards * 6 + 5, shards, stride=6), :]
        line = jnp.sum(terms, axis=0, keepdims=True)
        gram_ref[n * share : (n + 1) * share, :] = jnp.broadcast_to(line, (share, LANES))


def inverse_factor(spread):
    rank = spread.shape[0]
    share = rank // HALF_GROUPS
    row = lax.broadcasted_iota(jnp.int32, (rank, LANES), 0)
    lane = lax.broadcasted_iota(jnp.int32, (rank, LANES), 1)
    at = lane - rank * (row % share)
    cols = [
        jnp.broadcast_to(jnp.sum(jnp.where(at == j, spread, 0.0), axis=1, keepdims=True), (rank, LANES))
        for j in range(rank)
    ]
    right = jnp.where(row == lane, 1.0, 0.0)
    pivots = jnp.ones((rank, LANES), jnp.float32)
    for k in range(rank):
        pivot = cols[k][k : k + 1]
        pivots = jnp.where(row == k, pivot, pivots)
        factor = jnp.where(row > k, cols[k] * (1.0 / pivot), 0.0)
        for j in range(k + 1, rank):
            cols[j] = cols[j] - factor * cols[j][k : k + 1]
        right = right - factor * right[k : k + 1]
    return right * (1.0 / jnp.sqrt(pivots))


def half_block(left, half_ref, g_ref, f_ref, core, n, rank):
    width = g_ref.shape[2] // CORES // HALF_GROUPS
    tiles = width // LANES
    raw = jnp.concatenate(
        [half_ref[pl.ds(n * rank * tiles + i, rank, stride=tiles), :] for i in range(tiles)], axis=1
    )
    high, mid, low = split(raw)
    out = bf16_dot(left, jnp.concatenate([high, mid, high, low, high, mid], axis=0), 1, 0)
    cols = pl.ds(column_at(core, n, width), width)
    return out[:rank], (g_ref[0, :, cols] + f_ref[0, :, cols]) - out[rank:]


def own_half_kernel(replicas, gram_ref, half_ref, mean_ref, g_ref, f_ref, left_ref, po_ref, qf_ref, nf_ref):
    rank = mean_ref.shape[0]
    whole = inverse_factor(gram_ref[...])
    lower = whole[:, :rank]
    ortho = dot(lower, mean_ref[...], 1, 0)
    po_ref[...] = ortho
    scaled = lower * (1.0 / replicas)
    both = jnp.concatenate([scaled, dot(ortho, scaled, 0, 0)], axis=0)
    high, mid, low = split(both)
    left = jnp.concatenate([high, high, mid, high, low, mid], axis=1)
    left_ref[...] = left
    width = qf_ref.shape[1] // HALF_GROUPS
    core = lax.axis_index("core")
    for n in range(HALF_GROUPS):
        cols = slice(n * width, (n + 1) * width)
        qf_ref[:, cols], nf_ref[:, cols] = half_block(left, half_ref, g_ref, f_ref, core, n, rank)


def finish_kernel(
    left_ref, po_ref, qf_ref, nf_ref, half_ref, g_ref, f_ref, nf_hbm, po_hbm, qf_hbm, nf_buf, qf_buf, sems, half_sems
):
    rank = po_ref.shape[0]
    core = lax.axis_index("core")
    width = qf_ref.shape[1] // HALF_GROUPS
    own = pl.ds(column_at(core, 0, width), HALF_GROUPS * width)
    copies = [
        pltpu.make_async_copy(nf_ref, nf_hbm.at[0, :, own], half_sems.at[0]),
        pltpu.make_async_copy(qf_ref, qf_hbm.at[:, own], half_sems.at[1]),
        pltpu.make_async_copy(po_ref, po_hbm, half_sems.at[2]),
    ]
    for copy in copies:
        copy.start()
    left = left_ref[...]
    for n in range(HALF_GROUPS):
        cols = slice(n * width, (n + 1) * width)
        qf_buf[:, cols], nf_buf[:, cols] = half_block(left, half_ref, g_ref, f_ref, 1 - core, n, rank)
        here = pl.ds(n * width, width)
        there = pl.ds(column_at(1 - core, n, width), width)
        part = [
            pltpu.make_async_copy(nf_buf.at[:, here], nf_hbm.at[0, :, there], sems.at[0, n]),
            pltpu.make_async_copy(qf_buf.at[:, here], qf_hbm.at[:, there], sems.at[1, n]),
        ]
        for copy in part:
            copy.start()
        copies += part
    for copy in copies:
        copy.wait()


def body(gradient, feedback, q_previous):
    f32 = jnp.float32
    dp, mp = lax.axis_size(DP), lax.axis_size(MP)
    _, rows, width = gradient.shape
    rank = q_previous.shape[0]
    tiles = width // CORES // HALF_GROUPS // LANES
    vmem = pl.BlockSpec(memory_space=pltpu.VMEM)
    hbm = pl.BlockSpec(memory_space=pltpu.HBM)
    params = pltpu.CompilerParams(vmem_limit_bytes=16 * 2**20)

    p_out, c_send = pl.pallas_call(
        correct_kernel,
        in_specs=[hbm, hbm, hbm],
        out_specs=[vmem, hbm],
        out_shape=[
            jax.ShapeDtypeStruct((dp, rank // 2, 2 * rows), f32),
            jax.ShapeDtypeStruct((rows, width // CORES), f32),
        ],
        scratch_shapes=[
            pltpu.VMEM((rows, width), f32),
            pltpu.VMEM((rows, width), f32),
            pltpu.VMEM((rank, width), f32),
            pltpu.VMEM((rows, width // CORES), f32),
            pltpu.SemaphoreType.DMA((3, IN_PARTS)),
            pltpu.SemaphoreType.DMA((IN_PARTS // CORES,)),
        ],
        compiler_params=pltpu.CompilerParams(vmem_limit_bytes=int(53.75 * 2**20)),
        name="correct",
    )(gradient, feedback, q_previous)
    sizes = tuple(lax.axis_size(name) for name in DP + MP)
    near = [[member_of(i) * CORES + core for i in range(sizes[0]) for core in (1, 0)]]
    chips = chip_groups(sizes)
    arrived = lax.ppermute(c_send, "core", [(0, 1), (1, 0)])
    p_all = lax.all_to_all(p_out, DP, 0, 0, tiled=True, axis_index_groups=near)

    count = sizes[0] * mp
    msg, p_mean = pl.pallas_call(
        project_kernel,
        in_specs=[vmem] * 4,
        out_specs=[vmem] * 2,
        out_shape=[
            jax.ShapeDtypeStruct((count * (tiles + 1), LANES), f32),
            jax.ShapeDtypeStruct((rank, rows), f32),
        ],
        compiler_params=params,
        name="project",
    )(p_all, gradient, feedback, arrived)
    msg = msg.reshape(count, 1, (tiles + 1) * LANES)
    terms = lax.all_to_all(msg, DP + MP, 0, 0, tiled=True, axis_index_groups=chips)

    own, gram = pl.pallas_call(
        sum_kernel,
        in_specs=[vmem],
        out_specs=[vmem, vmem],
        out_shape=[
            jax.ShapeDtypeStruct((count * tiles, LANES), f32),
            jax.ShapeDtypeStruct((rank, LANES), f32),
        ],
        scratch_shapes=[pltpu.VMEM((24, LANES), f32)],
        compiler_params=params,
        name="sum_terms",
    )(terms.reshape(count * (tiles + 1), LANES))
    own = own.reshape(count, 1, tiles * LANES)
    half = lax.all_to_all(own, DP + MP, 0, 0, tiled=True, axis_index_groups=chips).reshape(count * tiles, LANES)
    other = lax.ppermute(half, "core", [(0, 1), (1, 0)])

    left, p_ortho, q_half, f_half = pl.pallas_call(
        functools.partial(own_half_kernel, dp),
        in_specs=[vmem] * 5,
        out_specs=[vmem] * 4,
        out_shape=[
            jax.ShapeDtypeStruct((rank + rows, 6 * rank), jnp.bfloat16),
            jax.ShapeDtypeStruct((rank, rows), f32),
            jax.ShapeDtypeStruct((rank, width // CORES), f32),
            jax.ShapeDtypeStruct((rows, width // CORES), f32),
        ],
        compiler_params=params,
        cost_estimate=pl.CostEstimate(flops=2 * rows * width * 96, bytes_accessed=8 * rows * width, transcendentals=0),
        name="own_half",
    )(gram, half, p_mean, gradient, feedback)
    new_feedback, p_ortho, q_factor = pl.pallas_call(
        finish_kernel,
        in_specs=[vmem] * 7,
        out_specs=[hbm] * 3,
        out_shape=[
            jax.ShapeDtypeStruct((1, rows, width), f32),
            jax.ShapeDtypeStruct((rank, rows), f32),
            jax.ShapeDtypeStruct((rank, width), f32),
        ],
        scratch_shapes=[
            pltpu.VMEM((rows, width // CORES), f32),
            pltpu.VMEM((rank, width // CORES), f32),
            pltpu.SemaphoreType.DMA((2, HALF_GROUPS)),
            pltpu.SemaphoreType.DMA((3,)),
        ],
        compiler_params=params,
        name="finish",
    )(left, p_ortho, q_half, f_half, other, gradient, feedback)
    return (new_feedback, p_ortho, q_factor)


def solution(mesh):
    sizes = (mesh.shape["dp"] // CORES, CORES, math.isqrt(mesh.shape["mp"]), math.isqrt(mesh.shape["mp"]))
    fine = jax.sharding.Mesh(mesh.devices.reshape(sizes), DP + MP)
    return jax.shard_map(
        body,
        mesh=fine,
        in_specs=(P(DP, MP, None), P(DP, MP, None), P()),
        out_specs=(P(DP, MP, None), P(None, MP), P()),
        check_vma=False,
    )
```

```python
import functools
import math

import jax
import jax.numpy as jnp
from jax import lax
from jax.experimental import pallas as pl
from jax.experimental.pallas import tpu as pltpu
from jax.sharding import PartitionSpec as P

LANES = 128
IN_PARTS = 4
IN_TILE = 256
CORES = 2
HALF_GROUPS = 4
DP = ("x", "core")
MP = ("z", "y")


def dot(left, right, left_dim, right_dim):
    return lax.dot_general(
        left,
        right,
        (((left_dim,), (right_dim,)), ((), ())),
        precision=lax.Precision.HIGHEST,
        preferred_element_type=jnp.float32,
    )


def split(x):
    high = x.astype(jnp.bfloat16)
    rest = x - high.astype(jnp.float32)
    mid = rest.astype(jnp.bfloat16)
    low = (rest - mid.astype(jnp.float32)).astype(jnp.bfloat16)
    return high, mid, low


def bf16_dot(left, right, left_dim, right_dim):
    return lax.dot_general(
        left, right, (((left_dim,), (right_dim,)), ((), ())), preferred_element_type=jnp.float32
    )


def fold(x, size, axis):
    parts = [lax.slice_in_dim(x, n * size, (n + 1) * size, axis=axis) for n in range(3)]
    return (parts[2] + parts[1]) + parts[0]


def correct_kernel(g_hbm, f_hbm, q_hbm, p_ref, c_hbm, g_buf, f_buf, q_buf, c_buf, sems, c_sems):
    half = c_buf.shape[1]
    parts = IN_PARTS // CORES
    width = half // parts
    core = half_of_core()
    copies = []
    for s in range(IN_PARTS):
        first = (1 - core if s < parts else core) * half + s % parts * width
        there = pl.ds(pl.multiple_of(first, width), width)
        here = pl.ds(s * width, width)
        part = [
            pltpu.make_async_copy(g_hbm.at[0, :, there], g_buf.at[:, here], sems.at[0, s]),
            pltpu.make_async_copy(f_hbm.at[0, :, there], f_buf.at[:, here], sems.at[1, s]),
            pltpu.make_async_copy(q_hbm.at[:, there], q_buf.at[:, here], sems.at[2, s]),
        ]
        for copy in part:
            copy.start()
        copies.append(part)
    total = None
    sends = []
    for s in range(IN_PARTS):
        for copy in copies[s]:
            copy.wait()
        for at in range(s * width, (s + 1) * width, IN_TILE):
            cols = slice(at, at + IN_TILE)
            local = g_buf[:, cols] + f_buf[:, cols]
            if s < parts:
                c_buf[:, cols] = local
            left = jnp.concatenate(split(q_buf[:, cols]), axis=0)
            right = jnp.concatenate(split(local), axis=0)
            part = bf16_dot(left, right, 1, 1)
            total = part if total is None else total + part
        if s < parts:
            cols = pl.ds(s * width, width)
            sends.append(pltpu.make_async_copy(c_buf.at[:, cols], c_hbm.at[:, cols], c_sems.at[s]))
            sends[-1].start()
    total = fold(fold(total, total.shape[0] // 3, 0), total.shape[1] // 3, 1)
    half = total.shape[0] // 2
    packed = jnp.concatenate([total[:half], total[half:]], axis=1)
    p_ref[...] = jnp.broadcast_to(packed[None], p_ref.shape)
    for copy in sends:
        copy.wait()


def member_of(place):
    return (6 - place) % 4


def chip_groups(sizes):
    nx, nc, nz, ny = sizes
    return [
        [
            ((member_of(i) * nc + (core ^ int(i + j + k == 0))) * nz + member_of(j)) * ny + member_of(k)
            for i in range(nx)
            for j in range(nz)
            for k in range(ny)
        ]
        for core in range(nc)
    ]


def half_of_core():
    core = lax.axis_index("core")
    leads = (lax.axis_index("x") == 2) & (lax.axis_index("z") == 2) & (lax.axis_index("y") == 2)
    return jnp.where(leads, 1 - core, core)


def column_at(core, n, width):
    return pl.multiple_of((core * HALF_GROUPS + n) * width, width)


def project_kernel(p_ref, g_ref, f_ref, arrived_ref, msg_ref, mean_ref):
    replicas = p_ref.shape[0]
    total = p_ref[0]
    for n in range(1, replicas):
        total = total + p_ref[n]
    total = total * (1.0 / replicas)
    half = total.shape[1] // 2
    mean = jnp.concatenate([total[:, :half], total[:, half:]], axis=0)
    mean_ref[...] = mean
    rank = mean.shape[0]
    high, mid, low = split(mean)
    none = jnp.zeros_like(high)
    left = jnp.concatenate(
        [jnp.concatenate(parts, axis=1) for parts in ((high, high, high), (mid, mid, none), (low, none, none))], axis=0
    )
    width = arrived_ref.shape[1] // HALF_GROUPS
    tiles = width // LANES
    for n in range(HALF_GROUPS):
        cols = pl.ds(column_at(half_of_core(), n, width), width)
        pair = (g_ref[0, :, cols] + f_ref[0, :, cols]) + arrived_ref[:, n * width : (n + 1) * width]
        out = fold(bf16_dot(left, jnp.concatenate(split(pair), axis=0), 1, 0), rank, 0)
        for i in range(tiles):
            first = n * rank * (tiles + 1) + i
            msg_ref[pl.ds(first, rank, stride=tiles + 1), :] = out[:, i * LANES : (i + 1) * LANES]
    gram = dot(mean, jnp.concatenate([mean] * (LANES // rank), axis=0), 1, 1)
    share = rank // HALF_GROUPS
    row = lax.broadcasted_iota(jnp.int32, (rank, LANES), 0)
    lane = lax.broadcasted_iota(jnp.int32, (rank, LANES), 1)
    mine = row - share * member_of(lax.axis_index("x"))
    kept = (lane >= rank * mine) & (lane < rank * (mine + 1)) & (mine >= 0) & (mine < share)
    line = jnp.sum(jnp.where(kept, gram, 0.0), axis=0, keepdims=True)
    count = msg_ref.shape[0] // (tiles + 1)
    msg_ref[pl.ds(tiles, count, stride=tiles + 1), :] = jnp.broadcast_to(line, (count, LANES))


def sum_kernel(in_ref, out_ref, gram_ref, part):
    peers = in_ref.shape[0] // 6
    total = in_ref[0:24]
    for s in range(1, peers // 4):
        total = total + in_ref[24 * s : 24 * (s + 1)]
    part[...] = total
    for i in range(5):
        line = jnp.sum(part[pl.ds(i, 4, stride=6), :], axis=0, keepdims=True)
        out_ref[pl.ds(i, peers, stride=5), :] = jnp.broadcast_to(line, (peers, LANES))
    shards = peers // HALF_GROUPS
    share = gram_ref.shape[0] // HALF_GROUPS
    for n in range(HALF_GROUPS):
        terms = in_ref[pl.ds(n * shards * 6 + 5, shards, stride=6), :]
        line = jnp.sum(terms, axis=0, keepdims=True)
        gram_ref[n * share : (n + 1) * share, :] = jnp.broadcast_to(line, (share, LANES))


def inverse_factor(spread):
    rank = spread.shape[0]
    share = rank // HALF_GROUPS
    row = lax.broadcasted_iota(jnp.int32, (rank, LANES), 0)
    lane = lax.broadcasted_iota(jnp.int32, (rank, LANES), 1)
    at = lane - rank * (row % share)
    cols = [
        jnp.broadcast_to(jnp.sum(jnp.where(at == j, spread, 0.0), axis=1, keepdims=True), (rank, LANES))
        for j in range(rank)
    ]
    right = jnp.where(row == lane, 1.0, 0.0)
    pivots = jnp.ones((rank, LANES), jnp.float32)
    for k in range(rank):
        pivot = cols[k][k : k + 1]
        pivots = jnp.where(row == k, pivot, pivots)
        factor = jnp.where(row > k, cols[k] * (1.0 / pivot), 0.0)
        for j in range(k + 1, rank):
            cols[j] = cols[j] - factor * cols[j][k : k + 1]
        right = right - factor * right[k : k + 1]
    return right * (1.0 / jnp.sqrt(pivots))


def half_block(left, half_ref, g_ref, f_ref, core, n, rank):
    width = g_ref.shape[2] // CORES // HALF_GROUPS
    tiles = width // LANES
    raw = jnp.concatenate(
        [half_ref[pl.ds(n * rank * tiles + i, rank, stride=tiles), :] for i in range(tiles)], axis=1
    )
    high, mid, low = split(raw)
    out = bf16_dot(left, jnp.concatenate([high, mid, high, low, high, mid], axis=0), 1, 0)
    cols = pl.ds(column_at(core, n, width), width)
    return out[:rank], (g_ref[0, :, cols] + f_ref[0, :, cols]) - out[rank:]


def own_half_kernel(replicas, gram_ref, half_ref, mean_ref, g_ref, f_ref, left_ref, po_ref, qf_ref, nf_ref):
    rank = mean_ref.shape[0]
    whole = inverse_factor(gram_ref[...])
    lower = whole[:, :rank]
    ortho = dot(lower, mean_ref[...], 1, 0)
    po_ref[...] = ortho
    scaled = lower * (1.0 / replicas)
    both = jnp.concatenate([scaled, dot(ortho, scaled, 0, 0)], axis=0)
    high, mid, low = split(both)
    left = jnp.concatenate([high, high, mid, high, low, mid], axis=1)
    left_ref[...] = left
    width = qf_ref.shape[1] // HALF_GROUPS
    core = half_of_core()
    for n in range(HALF_GROUPS):
        cols = slice(n * width, (n + 1) * width)
        qf_ref[:, cols], nf_ref[:, cols] = half_block(left, half_ref, g_ref, f_ref, core, n, rank)


def finish_kernel(
    left_ref, po_ref, qf_ref, nf_ref, half_ref, g_ref, f_ref, nf_hbm, po_hbm, qf_hbm, nf_buf, qf_buf, sems, half_sems
):
    rank = po_ref.shape[0]
    core = half_of_core()
    width = qf_ref.shape[1] // HALF_GROUPS
    own = pl.ds(column_at(core, 0, width), HALF_GROUPS * width)
    copies = [
        pltpu.make_async_copy(nf_ref, nf_hbm.at[0, :, own], half_sems.at[0]),
        pltpu.make_async_copy(qf_ref, qf_hbm.at[:, own], half_sems.at[1]),
        pltpu.make_async_copy(po_ref, po_hbm, half_sems.at[2]),
    ]
    for copy in copies:
        copy.start()
    left = left_ref[...]
    for n in range(HALF_GROUPS):
        cols = slice(n * width, (n + 1) * width)
        qf_buf[:, cols], nf_buf[:, cols] = half_block(left, half_ref, g_ref, f_ref, 1 - core, n, rank)
        here = pl.ds(n * width, width)
        there = pl.ds(column_at(1 - core, n, width), width)
        part = [
            pltpu.make_async_copy(nf_buf.at[:, here], nf_hbm.at[0, :, there], sems.at[0, n]),
            pltpu.make_async_copy(qf_buf.at[:, here], qf_hbm.at[:, there], sems.at[1, n]),
        ]
        for copy in part:
            copy.start()
        copies += part
    for copy in copies:
        copy.wait()


def body(gradient, feedback, q_previous):
    f32 = jnp.float32
    dp, mp = lax.axis_size(DP), lax.axis_size(MP)
    _, rows, width = gradient.shape
    rank = q_previous.shape[0]
    tiles = width // CORES // HALF_GROUPS // LANES
    vmem = pl.BlockSpec(memory_space=pltpu.VMEM)
    hbm = pl.BlockSpec(memory_space=pltpu.HBM)
    params = pltpu.CompilerParams(vmem_limit_bytes=16 * 2**20)

    p_out, c_send = pl.pallas_call(
        correct_kernel,
        in_specs=[hbm, hbm, hbm],
        out_specs=[vmem, hbm],
        out_shape=[
            jax.ShapeDtypeStruct((dp, rank // 2, 2 * rows), f32),
            jax.ShapeDtypeStruct((rows, width // CORES), f32),
        ],
        scratch_shapes=[
            pltpu.VMEM((rows, width), f32),
            pltpu.VMEM((rows, width), f32),
            pltpu.VMEM((rank, width), f32),
            pltpu.VMEM((rows, width // CORES), f32),
            pltpu.SemaphoreType.DMA((3, IN_PARTS)),
            pltpu.SemaphoreType.DMA((IN_PARTS // CORES,)),
        ],
        compiler_params=pltpu.CompilerParams(vmem_limit_bytes=int(53.75 * 2**20)),
        name="correct",
    )(gradient, feedback, q_previous)
    sizes = tuple(lax.axis_size(name) for name in DP + MP)
    near = [[member_of(i) * CORES + core for i in range(sizes[0]) for core in (0, 1)]]
    chips = chip_groups(sizes)
    chips[1][0], chips[1][12] = chips[1][12], chips[1][0]
    arrived = lax.ppermute(c_send, "core", [(0, 1), (1, 0)])
    p_all = lax.all_to_all(p_out, DP, 0, 0, tiled=True, axis_index_groups=near)

    count = sizes[0] * mp
    msg, p_mean = pl.pallas_call(
        project_kernel,
        in_specs=[vmem] * 4,
        out_specs=[vmem] * 2,
        out_shape=[
            jax.ShapeDtypeStruct((count * (tiles + 1), LANES), f32),
            jax.ShapeDtypeStruct((rank, rows), f32),
        ],
        compiler_params=params,
        name="project",
    )(p_all, gradient, feedback, arrived)
    msg = msg.reshape(count, 1, (tiles + 1) * LANES)
    terms = lax.all_to_all(msg, DP + MP, 0, 0, tiled=True, axis_index_groups=chips)

    own, gram = pl.pallas_call(
        sum_kernel,
        in_specs=[vmem],
        out_specs=[vmem, vmem],
        out_shape=[
            jax.ShapeDtypeStruct((count * tiles, LANES), f32),
            jax.ShapeDtypeStruct((rank, LANES), f32),
        ],
        scratch_shapes=[pltpu.VMEM((24, LANES), f32)],
        compiler_params=params,
        name="sum_terms",
    )(terms.reshape(count * (tiles + 1), LANES))
    own = own.reshape(count, 1, tiles * LANES)
    half = lax.all_to_all(own, DP + MP, 0, 0, tiled=True, axis_index_groups=chips).reshape(count * tiles, LANES)
    other = lax.ppermute(half, "core", [(0, 1), (1, 0)])

    left, p_ortho, q_half, f_half = pl.pallas_call(
        functools.partial(own_half_kernel, dp),
        in_specs=[vmem] * 5,
        out_specs=[vmem] * 4,
        out_shape=[
            jax.ShapeDtypeStruct((rank + rows, 6 * rank), jnp.bfloat16),
            jax.ShapeDtypeStruct((rank, rows), f32),
            jax.ShapeDtypeStruct((rank, width // CORES), f32),
            jax.ShapeDtypeStruct((rows, width // CORES), f32),
        ],
        compiler_params=params,
        cost_estimate=pl.CostEstimate(flops=2 * rows * width * 96, bytes_accessed=8 * rows * width, transcendentals=0),
        name="own_half",
    )(gram, half, p_mean, gradient, feedback)
    new_feedback, p_ortho, q_factor = pl.pallas_call(
        finish_kernel,
        in_specs=[vmem] * 7,
        out_specs=[hbm] * 3,
        out_shape=[
            jax.ShapeDtypeStruct((1, rows, width), f32),
            jax.ShapeDtypeStruct((rank, rows), f32),
            jax.ShapeDtypeStruct((rank, width), f32),
        ],
        scratch_shapes=[
            pltpu.VMEM((rows, width // CORES), f32),
            pltpu.VMEM((rank, width // CORES), f32),
            pltpu.SemaphoreType.DMA((2, HALF_GROUPS)),
            pltpu.SemaphoreType.DMA((3,)),
        ],
        compiler_params=params,
        name="finish",
    )(left, p_ortho, q_half, f_half, other, gradient, feedback)
    return (new_feedback, p_ortho, q_factor)


def solution(mesh):
    sizes = (mesh.shape["dp"] // CORES, CORES, math.isqrt(mesh.shape["mp"]), math.isqrt(mesh.shape["mp"]))
    fine = jax.sharding.Mesh(mesh.devices.reshape(sizes), DP + MP)
    return jax.shard_map(
        body,
        mesh=fine,
        in_specs=(P(DP, MP, None), P(DP, MP, None), P()),
        out_specs=(P(DP, MP, None), P(None, MP), P()),
        check_vma=False,
    )
```

```python
import functools
import math

import jax
import jax.numpy as jnp
from jax import lax
from jax.experimental import pallas as pl
from jax.experimental.pallas import tpu as pltpu
from jax.sharding import PartitionSpec as P

LANES = 128
IN_PARTS = 4
IN_TILE = 256
CORES = 2
HALF_GROUPS = 4
DP = ("x", "core")
MP = ("z", "y")


def dot(left, right, left_dim, right_dim):
    return lax.dot_general(
        left,
        right,
        (((left_dim,), (right_dim,)), ((), ())),
        precision=lax.Precision.HIGHEST,
        preferred_element_type=jnp.float32,
    )


def split(x):
    high = x.astype(jnp.bfloat16)
    rest = x - high.astype(jnp.float32)
    mid = rest.astype(jnp.bfloat16)
    low = (rest - mid.astype(jnp.float32)).astype(jnp.bfloat16)
    return high, mid, low


def bf16_dot(left, right, left_dim, right_dim):
    return lax.dot_general(
        left, right, (((left_dim,), (right_dim,)), ((), ())), preferred_element_type=jnp.float32
    )


def fold(x, size, axis):
    parts = [lax.slice_in_dim(x, n * size, (n + 1) * size, axis=axis) for n in range(3)]
    return (parts[2] + parts[1]) + parts[0]


def correct_kernel(g_hbm, f_hbm, q_hbm, p_ref, c_hbm, g_buf, f_buf, q_buf, c_buf, sems, c_sems):
    half = c_buf.shape[1]
    parts = IN_PARTS // CORES
    width = half // parts
    core = half_of_core()
    copies = []
    for s in range(IN_PARTS):
        first = (1 - core if s < parts else core) * half + s % parts * width
        there = pl.ds(pl.multiple_of(first, width), width)
        here = pl.ds(s * width, width)
        part = [
            pltpu.make_async_copy(g_hbm.at[0, :, there], g_buf.at[:, here], sems.at[0, s]),
            pltpu.make_async_copy(f_hbm.at[0, :, there], f_buf.at[:, here], sems.at[1, s]),
            pltpu.make_async_copy(q_hbm.at[:, there], q_buf.at[:, here], sems.at[2, s]),
        ]
        for copy in part:
            copy.start()
        copies.append(part)
    total = None
    sends = []
    for s in range(IN_PARTS):
        for copy in copies[s]:
            copy.wait()
        for at in range(s * width, (s + 1) * width, IN_TILE):
            cols = slice(at, at + IN_TILE)
            local = g_buf[:, cols] + f_buf[:, cols]
            if s < parts:
                c_buf[:, cols] = local
            left = jnp.concatenate(split(q_buf[:, cols]), axis=0)
            right = jnp.concatenate(split(local), axis=0)
            part = bf16_dot(left, right, 1, 1)
            total = part if total is None else total + part
        if s < parts:
            cols = pl.ds(s * width, width)
            sends.append(pltpu.make_async_copy(c_buf.at[:, cols], c_hbm.at[:, cols], c_sems.at[s]))
            sends[-1].start()
    total = fold(fold(total, total.shape[0] // 3, 0), total.shape[1] // 3, 1)
    half = total.shape[0] // 2
    packed = jnp.concatenate([total[:half], total[half:]], axis=1)
    p_ref[...] = jnp.broadcast_to(packed[None], p_ref.shape)
    for copy in sends:
        copy.wait()


def member_of(place):
    return (6 - place) % 4


def chip_groups(sizes):
    nx, nc, nz, ny = sizes
    return [
        [
            ((member_of(i) * nc + (core ^ int((member_of(i), z, member_of(k)) == (2, 2, 2)))) * nz + z) * ny + member_of(k)
            for i in range(nx)
            for z in (2, 1, 3, 0)
            for k in range(ny)
        ]
        for core in range(nc)
    ]


def half_of_core():
    core = lax.axis_index("core")
    leads = (lax.axis_index("x") == 2) & (lax.axis_index("z") == 2) & (lax.axis_index("y") == 2)
    return jnp.where(leads, 1 - core, core)


def column_at(core, n, width):
    return pl.multiple_of((core * HALF_GROUPS + n) * width, width)


def project_kernel(p_ref, g_ref, f_ref, arrived_ref, msg_ref, mean_ref):
    replicas = p_ref.shape[0]
    total = p_ref[0]
    for n in range(1, replicas):
        total = total + p_ref[n]
    total = total * (1.0 / replicas)
    half = total.shape[1] // 2
    mean = jnp.concatenate([total[:, :half], total[:, half:]], axis=0)
    mean_ref[...] = mean
    rank = mean.shape[0]
    high, mid, low = split(mean)
    none = jnp.zeros_like(high)
    left = jnp.concatenate(
        [jnp.concatenate(parts, axis=1) for parts in ((high, high, high), (mid, mid, none), (low, none, none))], axis=0
    )
    width = arrived_ref.shape[1] // HALF_GROUPS
    tiles = width // LANES
    for n in range(HALF_GROUPS):
        cols = pl.ds(column_at(half_of_core(), n, width), width)
        pair = (g_ref[0, :, cols] + f_ref[0, :, cols]) + arrived_ref[:, n * width : (n + 1) * width]
        out = fold(bf16_dot(left, jnp.concatenate(split(pair), axis=0), 1, 0), rank, 0)
        for i in range(tiles):
            first = n * rank * (tiles + 1) + i
            msg_ref[pl.ds(first, rank, stride=tiles + 1), :] = out[:, i * LANES : (i + 1) * LANES]
    gram = dot(mean, jnp.concatenate([mean] * (LANES // rank), axis=0), 1, 1)
    share = rank // HALF_GROUPS
    row = lax.broadcasted_iota(jnp.int32, (rank, LANES), 0)
    lane = lax.broadcasted_iota(jnp.int32, (rank, LANES), 1)
    mine = row - share * member_of(lax.axis_index("x"))
    kept = (lane >= rank * mine) & (lane < rank * (mine + 1)) & (mine >= 0) & (mine < share)
    line = jnp.sum(jnp.where(kept, gram, 0.0), axis=0, keepdims=True)
    count = msg_ref.shape[0] // (tiles + 1)
    msg_ref[pl.ds(tiles, count, stride=tiles + 1), :] = jnp.broadcast_to(line, (count, LANES))


def sum_kernel(in_ref, out_ref, gram_ref, part):
    peers = in_ref.shape[0] // 6
    total = in_ref[0:24]
    for s in range(1, peers // 4):
        total = total + in_ref[24 * s : 24 * (s + 1)]
    part[...] = total
    for i in range(5):
        line = jnp.sum(part[pl.ds(i, 4, stride=6), :], axis=0, keepdims=True)
        out_ref[pl.ds(i, peers, stride=5), :] = jnp.broadcast_to(line, (peers, LANES))
    shards = peers // HALF_GROUPS
    share = gram_ref.shape[0] // HALF_GROUPS
    for n in range(HALF_GROUPS):
        terms = in_ref[pl.ds(n * shards * 6 + 5, shards, stride=6), :]
        line = jnp.sum(terms, axis=0, keepdims=True)
        gram_ref[n * share : (n + 1) * share, :] = jnp.broadcast_to(line, (share, LANES))


def inverse_factor(spread):
    rank = spread.shape[0]
    share = rank // HALF_GROUPS
    row = lax.broadcasted_iota(jnp.int32, (rank, LANES), 0)
    lane = lax.broadcasted_iota(jnp.int32, (rank, LANES), 1)
    at = lane - rank * (row % share)
    cols = [
        jnp.broadcast_to(jnp.sum(jnp.where(at == j, spread, 0.0), axis=1, keepdims=True), (rank, LANES))
        for j in range(rank)
    ]
    right = jnp.where(row == lane, 1.0, 0.0)
    pivots = jnp.ones((rank, LANES), jnp.float32)
    for k in range(rank):
        pivot = cols[k][k : k + 1]
        pivots = jnp.where(row == k, pivot, pivots)
        factor = jnp.where(row > k, cols[k] * (1.0 / pivot), 0.0)
        for j in range(k + 1, rank):
            cols[j] = cols[j] - factor * cols[j][k : k + 1]
        right = right - factor * right[k : k + 1]
    return right * (1.0 / jnp.sqrt(pivots))


def half_block(left, half_ref, g_ref, f_ref, core, n, rank):
    width = g_ref.shape[2] // CORES // HALF_GROUPS
    tiles = width // LANES
    raw = jnp.concatenate(
        [half_ref[pl.ds(n * rank * tiles + i, rank, stride=tiles), :] for i in range(tiles)], axis=1
    )
    high, mid, low = split(raw)
    out = bf16_dot(left, jnp.concatenate([high, mid, high, low, high, mid], axis=0), 1, 0)
    cols = pl.ds(column_at(core, n, width), width)
    return out[:rank], (g_ref[0, :, cols] + f_ref[0, :, cols]) - out[rank:]


def own_half_kernel(replicas, gram_ref, half_ref, mean_ref, g_ref, f_ref, left_ref, po_ref, qf_ref, nf_ref):
    rank = mean_ref.shape[0]
    whole = inverse_factor(gram_ref[...])
    lower = whole[:, :rank]
    ortho = dot(lower, mean_ref[...], 1, 0)
    po_ref[...] = ortho
    scaled = lower * (1.0 / replicas)
    both = jnp.concatenate([scaled, dot(ortho, scaled, 0, 0)], axis=0)
    high, mid, low = split(both)
    left = jnp.concatenate([high, high, mid, high, low, mid], axis=1)
    left_ref[...] = left
    width = qf_ref.shape[1] // HALF_GROUPS
    core = half_of_core()
    for n in range(HALF_GROUPS):
        cols = slice(n * width, (n + 1) * width)
        qf_ref[:, cols], nf_ref[:, cols] = half_block(left, half_ref, g_ref, f_ref, core, n, rank)


def finish_kernel(
    left_ref, po_ref, qf_ref, nf_ref, half_ref, g_ref, f_ref, nf_hbm, po_hbm, qf_hbm, nf_buf, qf_buf, sems, half_sems
):
    rank = po_ref.shape[0]
    core = half_of_core()
    width = qf_ref.shape[1] // HALF_GROUPS
    own = pl.ds(column_at(core, 0, width), HALF_GROUPS * width)
    copies = [
        pltpu.make_async_copy(nf_ref, nf_hbm.at[0, :, own], half_sems.at[0]),
        pltpu.make_async_copy(qf_ref, qf_hbm.at[:, own], half_sems.at[1]),
        pltpu.make_async_copy(po_ref, po_hbm, half_sems.at[2]),
    ]
    for copy in copies:
        copy.start()
    left = left_ref[...]
    for n in range(HALF_GROUPS):
        cols = slice(n * width, (n + 1) * width)
        qf_buf[:, cols], nf_buf[:, cols] = half_block(left, half_ref, g_ref, f_ref, 1 - core, n, rank)
        here = pl.ds(n * width, width)
        there = pl.ds(column_at(1 - core, n, width), width)
        part = [
            pltpu.make_async_copy(nf_buf.at[:, here], nf_hbm.at[0, :, there], sems.at[0, n]),
            pltpu.make_async_copy(qf_buf.at[:, here], qf_hbm.at[:, there], sems.at[1, n]),
        ]
        for copy in part:
            copy.start()
        copies += part
    for copy in copies:
        copy.wait()


def body(gradient, feedback, q_previous):
    f32 = jnp.float32
    dp, mp = lax.axis_size(DP), lax.axis_size(MP)
    _, rows, width = gradient.shape
    rank = q_previous.shape[0]
    tiles = width // CORES // HALF_GROUPS // LANES
    vmem = pl.BlockSpec(memory_space=pltpu.VMEM)
    hbm = pl.BlockSpec(memory_space=pltpu.HBM)
    params = pltpu.CompilerParams(vmem_limit_bytes=16 * 2**20)

    p_out, c_send = pl.pallas_call(
        correct_kernel,
        in_specs=[hbm, hbm, hbm],
        out_specs=[vmem, hbm],
        out_shape=[
            jax.ShapeDtypeStruct((dp, rank // 2, 2 * rows), f32),
            jax.ShapeDtypeStruct((rows, width // CORES), f32),
        ],
        scratch_shapes=[
            pltpu.VMEM((rows, width), f32),
            pltpu.VMEM((rows, width), f32),
            pltpu.VMEM((rank, width), f32),
            pltpu.VMEM((rows, width // CORES), f32),
            pltpu.SemaphoreType.DMA((3, IN_PARTS)),
            pltpu.SemaphoreType.DMA((IN_PARTS // CORES,)),
        ],
        compiler_params=pltpu.CompilerParams(vmem_limit_bytes=int(53.75 * 2**20)),
        name="correct",
    )(gradient, feedback, q_previous)
    sizes = tuple(lax.axis_size(name) for name in DP + MP)
    near = [[member_of(i) * CORES + core for i in range(sizes[0]) for core in (0, 1)]]
    chips = chip_groups(sizes)
    chips[1][0], chips[1][8] = chips[1][8], chips[1][0]
    arrived = lax.ppermute(c_send, "core", [(0, 1), (1, 0)])
    p_all = lax.all_to_all(p_out, DP, 0, 0, tiled=True, axis_index_groups=near)

    count = sizes[0] * mp
    msg, p_mean = pl.pallas_call(
        project_kernel,
        in_specs=[vmem] * 4,
        out_specs=[vmem] * 2,
        out_shape=[
            jax.ShapeDtypeStruct((count * (tiles + 1), LANES), f32),
            jax.ShapeDtypeStruct((rank, rows), f32),
        ],
        compiler_params=params,
        name="project",
    )(p_all, gradient, feedback, arrived)
    msg = msg.reshape(count, 1, (tiles + 1) * LANES)
    terms = lax.all_to_all(msg, DP + MP, 0, 0, tiled=True, axis_index_groups=chips)

    own, gram = pl.pallas_call(
        sum_kernel,
        in_specs=[vmem],
        out_specs=[vmem, vmem],
        out_shape=[
            jax.ShapeDtypeStruct((count * tiles, LANES), f32),
            jax.ShapeDtypeStruct((rank, LANES), f32),
        ],
        scratch_shapes=[pltpu.VMEM((24, LANES), f32)],
        compiler_params=params,
        name="sum_terms",
    )(terms.reshape(count * (tiles + 1), LANES))
    own = own.reshape(count, 1, tiles * LANES)
    half = lax.all_to_all(own, DP + MP, 0, 0, tiled=True, axis_index_groups=chips).reshape(count * tiles, LANES)
    other = lax.ppermute(half, "core", [(0, 1), (1, 0)])

    left, p_ortho, q_half, f_half = pl.pallas_call(
        functools.partial(own_half_kernel, dp),
        in_specs=[vmem] * 5,
        out_specs=[vmem] * 4,
        out_shape=[
            jax.ShapeDtypeStruct((rank + rows, 6 * rank), jnp.bfloat16),
            jax.ShapeDtypeStruct((rank, rows), f32),
            jax.ShapeDtypeStruct((rank, width // CORES), f32),
            jax.ShapeDtypeStruct((rows, width // CORES), f32),
        ],
        compiler_params=params,
        cost_estimate=pl.CostEstimate(flops=2 * rows * width * 96, bytes_accessed=8 * rows * width, transcendentals=0),
        name="own_half",
    )(gram, half, p_mean, gradient, feedback)
    new_feedback, p_ortho, q_factor = pl.pallas_call(
        finish_kernel,
        in_specs=[vmem] * 7,
        out_specs=[hbm] * 3,
        out_shape=[
            jax.ShapeDtypeStruct((1, rows, width), f32),
            jax.ShapeDtypeStruct((rank, rows), f32),
            jax.ShapeDtypeStruct((rank, width), f32),
        ],
        scratch_shapes=[
            pltpu.VMEM((rows, width // CORES), f32),
            pltpu.VMEM((rank, width // CORES), f32),
            pltpu.SemaphoreType.DMA((2, HALF_GROUPS)),
            pltpu.SemaphoreType.DMA((3,)),
        ],
        compiler_params=params,
        name="finish",
    )(left, p_ortho, q_half, f_half, other, gradient, feedback)
    return (new_feedback, p_ortho, q_factor)


def solution(mesh):
    sizes = (mesh.shape["dp"] // CORES, CORES, math.isqrt(mesh.shape["mp"]), math.isqrt(mesh.shape["mp"]))
    fine = jax.sharding.Mesh(mesh.devices.reshape(sizes), DP + MP)
    return jax.shard_map(
        body,
        mesh=fine,
        in_specs=(P(DP, MP, None), P(DP, MP, None), P()),
        out_specs=(P(DP, MP, None), P(None, MP), P()),
        check_vma=False,
    )
```

```python
import functools
import math

import jax
import jax.numpy as jnp
from jax import lax
from jax.experimental import pallas as pl
from jax.experimental.pallas import tpu as pltpu
from jax.sharding import PartitionSpec as P

LANES = 128
IN_PARTS = 4
IN_TILE = 256
CORES = 2
HALF_GROUPS = 2
BLOCKS = 4
DP = ("x", "core")
MP = ("z", "y")


def dot(left, right, left_dim, right_dim):
    return lax.dot_general(
        left,
        right,
        (((left_dim,), (right_dim,)), ((), ())),
        precision=lax.Precision.HIGHEST,
        preferred_element_type=jnp.float32,
    )


def split(x):
    high = x.astype(jnp.bfloat16)
    rest = x - high.astype(jnp.float32)
    mid = rest.astype(jnp.bfloat16)
    low = (rest - mid.astype(jnp.float32)).astype(jnp.bfloat16)
    return high, mid, low


def bf16_dot(left, right, left_dim, right_dim):
    return lax.dot_general(
        left, right, (((left_dim,), (right_dim,)), ((), ())), preferred_element_type=jnp.float32
    )


def fold(x, size, axis):
    parts = [lax.slice_in_dim(x, n * size, (n + 1) * size, axis=axis) for n in range(3)]
    return (parts[2] + parts[1]) + parts[0]


def correct_kernel(g_hbm, f_hbm, q_hbm, p_ref, c_hbm, g_buf, f_buf, q_buf, c_buf, sems, c_sems):
    half = c_buf.shape[1]
    parts = IN_PARTS // CORES
    width = half // parts
    core = half_of_core()
    copies = []
    for s in range(IN_PARTS):
        first = (1 - core if s < parts else core) * half + s % parts * width
        there = pl.ds(pl.multiple_of(first, width), width)
        here = pl.ds(s * width, width)
        part = [
            pltpu.make_async_copy(g_hbm.at[0, :, there], g_buf.at[:, here], sems.at[0, s]),
            pltpu.make_async_copy(f_hbm.at[0, :, there], f_buf.at[:, here], sems.at[1, s]),
            pltpu.make_async_copy(q_hbm.at[:, there], q_buf.at[:, here], sems.at[2, s]),
        ]
        for copy in part:
            copy.start()
        copies.append(part)
    total = None
    sends = []
    for s in range(IN_PARTS):
        for copy in copies[s]:
            copy.wait()
        for at in range(s * width, (s + 1) * width, IN_TILE):
            cols = slice(at, at + IN_TILE)
            local = g_buf[:, cols] + f_buf[:, cols]
            if s < parts:
                c_buf[:, cols] = local
            left = jnp.concatenate(split(q_buf[:, cols]), axis=0)
            right = jnp.concatenate(split(local), axis=0)
            part = bf16_dot(left, right, 1, 1)
            total = part if total is None else total + part
        if s < parts:
            cols = pl.ds(s * width, width)
            sends.append(pltpu.make_async_copy(c_buf.at[:, cols], c_hbm.at[:, cols], c_sems.at[s]))
            sends[-1].start()
    total = fold(fold(total, total.shape[0] // 3, 0), total.shape[1] // 3, 1)
    half = total.shape[0] // 2
    packed = jnp.concatenate([total[:half], total[half:]], axis=1)
    p_ref[...] = jnp.broadcast_to(packed[None], p_ref.shape)
    for copy in sends:
        copy.wait()


def chip_groups(sizes):
    nx, nc, nz, ny = sizes
    groups = []
    for group in range(nc):
        for half in ((2, 1), (3, 0)):
            groups.append([
                ((x * nc + (group ^ int((x, z, y) == (2, 2, 2)))) * nz + z) * ny + y
                for x in half
                for z in (2, 1, 3, 0)
                for y in (2, 1, 0, 3)
            ])
    groups[2][0], groups[2][8] = groups[2][8], groups[2][0]
    return groups


def half_of_core():
    core = lax.axis_index("core")
    leads = (lax.axis_index("x") == 2) & (lax.axis_index("z") == 2) & (lax.axis_index("y") == 2)
    return jnp.where(leads, 1 - core, core)


def column_at(core, block, width):
    return pl.multiple_of((core * BLOCKS + block) * width, width)


def first_row(block, rank, tiles, length):
    per_group = BLOCKS // HALF_GROUPS
    return block // per_group * rank * length + block % per_group * tiles


def project_kernel(p_ref, g_ref, f_ref, arrived_ref, msg_ref, mean_ref):
    replicas = p_ref.shape[0]
    total = p_ref[0]
    for n in range(1, replicas):
        total = total + p_ref[n]
    total = total * (1.0 / replicas)
    half = total.shape[1] // 2
    mean = jnp.concatenate([total[:, :half], total[:, half:]], axis=0)
    mean_ref[...] = mean
    rank = mean.shape[0]
    high, mid, low = split(mean)
    none = jnp.zeros_like(high)
    left = jnp.concatenate(
        [jnp.concatenate(parts, axis=1) for parts in ((high, high, high), (mid, mid, none), (low, none, none))], axis=0
    )
    width = arrived_ref.shape[1] // BLOCKS
    tiles = width // LANES
    length = BLOCKS // HALF_GROUPS * tiles + 1
    for n in range(BLOCKS):
        cols = pl.ds(column_at(half_of_core(), n, width), width)
        pair = (g_ref[0, :, cols] + f_ref[0, :, cols]) + arrived_ref[:, n * width : (n + 1) * width]
        out = fold(bf16_dot(left, jnp.concatenate(split(pair), axis=0), 1, 0), rank, 0)
        for i in range(tiles):
            first = first_row(n, rank, tiles, length) + i
            for at in (first, first + msg_ref.shape[0] // 2):
                msg_ref[pl.ds(at, rank, stride=length), :] = out[:, i * LANES : (i + 1) * LANES]
    gram = dot(mean, jnp.concatenate([mean] * (LANES // rank), axis=0), 1, 1)
    share = rank // HALF_GROUPS
    row = lax.broadcasted_iota(jnp.int32, (rank, LANES), 0)
    lane = lax.broadcasted_iota(jnp.int32, (rank, LANES), 1)
    mine = row - share * jnp.where(lax.axis_index("x") < 2, 1, 0)
    kept = (lane >= rank * mine) & (lane < rank * (mine + 1)) & (mine >= 0) & (mine < share)
    line = jnp.sum(jnp.where(kept, gram, 0.0), axis=0, keepdims=True)
    count = msg_ref.shape[0] // length
    msg_ref[pl.ds(length - 1, count, stride=length), :] = jnp.broadcast_to(line, (count, LANES))


def sum_kernel(in_ref, out_ref, gram_ref, part):
    members = HALF_GROUPS * gram_ref.shape[0]
    length = in_ref.shape[0] // (2 * members)
    rows = part.shape[0]
    total = in_ref[0:rows]
    for s in range(1, in_ref.shape[0] // rows):
        total = total + in_ref[rows * s : rows * (s + 1)]
    part[...] = total
    copies = out_ref.shape[0] // (length - 1)
    for i in range(length - 1):
        line = jnp.sum(part[pl.ds(i, rows // length, stride=length), :], axis=0, keepdims=True)
        out_ref[pl.ds(i, copies, stride=length - 1), :] = jnp.broadcast_to(line, (copies, LANES))
    shards = members // HALF_GROUPS
    share = gram_ref.shape[0] // HALF_GROUPS
    for n in range(HALF_GROUPS):
        terms = in_ref[pl.ds(n * shards * length + length - 1, shards, stride=length), :]
        line = jnp.sum(terms, axis=0, keepdims=True)
        gram_ref[n * share : (n + 1) * share, :] = jnp.broadcast_to(line, (share, LANES))


def inverse_factor(spread):
    rank = spread.shape[0]
    share = rank // HALF_GROUPS
    row = lax.broadcasted_iota(jnp.int32, (rank, LANES), 0)
    lane = lax.broadcasted_iota(jnp.int32, (rank, LANES), 1)
    at = lane - rank * (row % share)
    cols = [
        jnp.broadcast_to(jnp.sum(jnp.where(at == j, spread, 0.0), axis=1, keepdims=True), (rank, LANES))
        for j in range(rank)
    ]
    right = jnp.where(row == lane, 1.0, 0.0)
    pivots = jnp.ones((rank, LANES), jnp.float32)
    for k in range(rank):
        pivot = cols[k][k : k + 1]
        pivots = jnp.where(row == k, pivot, pivots)
        factor = jnp.where(row > k, cols[k] * (1.0 / pivot), 0.0)
        for j in range(k + 1, rank):
            cols[j] = cols[j] - factor * cols[j][k : k + 1]
        right = right - factor * right[k : k + 1]
    return right * (1.0 / jnp.sqrt(pivots))


def half_block(left, half_ref, g_ref, f_ref, core, n, rank):
    width = g_ref.shape[2] // CORES // BLOCKS
    tiles = width // LANES
    length = BLOCKS // HALF_GROUPS * tiles
    first = first_row(n, rank, tiles, length)
    raw = jnp.concatenate([half_ref[pl.ds(first + i, rank, stride=length), :] for i in range(tiles)], axis=1)
    high, mid, low = split(raw)
    out = bf16_dot(left, jnp.concatenate([high, mid, high, low, high, mid], axis=0), 1, 0)
    cols = pl.ds(column_at(core, n, width), width)
    return out[:rank], (g_ref[0, :, cols] + f_ref[0, :, cols]) - out[rank:]


def own_half_kernel(replicas, gram_ref, half_ref, mean_ref, g_ref, f_ref, left_ref, po_ref, qf_ref, nf_ref):
    rank = mean_ref.shape[0]
    whole = inverse_factor(gram_ref[...])
    lower = whole[:, :rank]
    ortho = dot(lower, mean_ref[...], 1, 0)
    po_ref[...] = ortho
    scaled = lower * (1.0 / replicas)
    both = jnp.concatenate([scaled, dot(ortho, scaled, 0, 0)], axis=0)
    high, mid, low = split(both)
    left = jnp.concatenate([high, high, mid, high, low, mid], axis=1)
    left_ref[...] = left
    width = qf_ref.shape[1] // BLOCKS
    core = half_of_core()
    for n in range(BLOCKS):
        cols = slice(n * width, (n + 1) * width)
        qf_ref[:, cols], nf_ref[:, cols] = half_block(left, half_ref, g_ref, f_ref, core, n, rank)


def finish_kernel(
    left_ref, po_ref, qf_ref, nf_ref, half_ref, g_ref, f_ref, nf_hbm, po_hbm, qf_hbm, nf_buf, qf_buf, sems, half_sems
):
    rank = po_ref.shape[0]
    core = half_of_core()
    width = qf_ref.shape[1] // BLOCKS
    own = pl.ds(column_at(core, 0, width), BLOCKS * width)
    copies = [
        pltpu.make_async_copy(nf_ref, nf_hbm.at[0, :, own], half_sems.at[0]),
        pltpu.make_async_copy(qf_ref, qf_hbm.at[:, own], half_sems.at[1]),
        pltpu.make_async_copy(po_ref, po_hbm, half_sems.at[2]),
    ]
    for copy in copies:
        copy.start()
    left = left_ref[...]
    for n in range(BLOCKS):
        cols = slice(n * width, (n + 1) * width)
        qf_buf[:, cols], nf_buf[:, cols] = half_block(left, half_ref, g_ref, f_ref, 1 - core, n, rank)
        here = pl.ds(n * width, width)
        there = pl.ds(column_at(1 - core, n, width), width)
        part = [
            pltpu.make_async_copy(nf_buf.at[:, here], nf_hbm.at[0, :, there], sems.at[0, n]),
            pltpu.make_async_copy(qf_buf.at[:, here], qf_hbm.at[:, there], sems.at[1, n]),
        ]
        for copy in part:
            copy.start()
        copies += part
    for copy in copies:
        copy.wait()


def body(gradient, feedback, q_previous):
    f32 = jnp.float32
    dp, mp = lax.axis_size(DP), lax.axis_size(MP)
    _, rows, width = gradient.shape
    rank = q_previous.shape[0]
    tiles = width // CORES // HALF_GROUPS // LANES
    members = HALF_GROUPS * rank
    vmem = pl.BlockSpec(memory_space=pltpu.VMEM)
    hbm = pl.BlockSpec(memory_space=pltpu.HBM)
    params = pltpu.CompilerParams(vmem_limit_bytes=16 * 2**20)

    p_out, c_send = pl.pallas_call(
        correct_kernel,
        in_specs=[hbm, hbm, hbm],
        out_specs=[vmem, hbm],
        out_shape=[
            jax.ShapeDtypeStruct((dp, rank // 2, 2 * rows), f32),
            jax.ShapeDtypeStruct((rows, width // CORES), f32),
        ],
        scratch_shapes=[
            pltpu.VMEM((rows, width), f32),
            pltpu.VMEM((rows, width), f32),
            pltpu.VMEM((rank, width), f32),
            pltpu.VMEM((rows, width // CORES), f32),
            pltpu.SemaphoreType.DMA((3, IN_PARTS)),
            pltpu.SemaphoreType.DMA((IN_PARTS // CORES,)),
        ],
        compiler_params=pltpu.CompilerParams(vmem_limit_bytes=int(53.75 * 2**20)),
        name="correct",
    )(gradient, feedback, q_previous)
    sizes = tuple(lax.axis_size(name) for name in DP + MP)
    near = [[x * CORES + core for x in (2, 1, 0, 3) for core in (0, 1)]]
    halves = chip_groups(sizes)
    chips = [halves[2 * n] + halves[2 * n + 1] for n in range(CORES)]
    arrived = lax.ppermute(c_send, "core", [(0, 1), (1, 0)])
    p_all = lax.all_to_all(p_out, DP, 0, 0, tiled=True, axis_index_groups=near)

    count = sizes[0] * mp
    msg, p_mean = pl.pallas_call(
        project_kernel,
        in_specs=[vmem] * 4,
        out_specs=[vmem] * 2,
        out_shape=[
            jax.ShapeDtypeStruct((count * (tiles + 1), LANES), f32),
            jax.ShapeDtypeStruct((rank, rows), f32),
        ],
        compiler_params=params,
        name="project",
    )(p_all, gradient, feedback, arrived)
    msg = msg.reshape(count, 1, (tiles + 1) * LANES)
    terms = lax.all_to_all(msg, DP + MP, 0, 0, tiled=True, axis_index_groups=chips)

    own, gram = pl.pallas_call(
        sum_kernel,
        in_specs=[vmem],
        out_specs=[vmem, vmem],
        out_shape=[
            jax.ShapeDtypeStruct((members * tiles, LANES), f32),
            jax.ShapeDtypeStruct((rank, LANES), f32),
        ],
        scratch_shapes=[pltpu.VMEM((8 * (tiles + 1), LANES), f32)],
        compiler_params=params,
        name="sum_terms",
    )(terms.reshape(count * (tiles + 1), LANES))
    own = own.reshape(members, 1, tiles * LANES)
    half = lax.all_to_all(own, DP + MP, 0, 0, tiled=True, axis_index_groups=halves).reshape(members * tiles, LANES)
    other = lax.ppermute(half, "core", [(0, 1), (1, 0)])

    left, p_ortho, q_half, f_half = pl.pallas_call(
        functools.partial(own_half_kernel, dp),
        in_specs=[vmem] * 5,
        out_specs=[vmem] * 4,
        out_shape=[
            jax.ShapeDtypeStruct((rank + rows, 6 * rank), jnp.bfloat16),
            jax.ShapeDtypeStruct((rank, rows), f32),
            jax.ShapeDtypeStruct((rank, width // CORES), f32),
            jax.ShapeDtypeStruct((rows, width // CORES), f32),
        ],
        compiler_params=params,
        cost_estimate=pl.CostEstimate(flops=2 * rows * width * 96, bytes_accessed=8 * rows * width, transcendentals=0),
        name="own_half",
    )(gram, half, p_mean, gradient, feedback)
    new_feedback, p_ortho, q_factor = pl.pallas_call(
        finish_kernel,
        in_specs=[vmem] * 7,
        out_specs=[hbm] * 3,
        out_shape=[
            jax.ShapeDtypeStruct((1, rows, width), f32),
            jax.ShapeDtypeStruct((rank, rows), f32),
            jax.ShapeDtypeStruct((rank, width), f32),
        ],
        scratch_shapes=[
            pltpu.VMEM((rows, width // CORES), f32),
            pltpu.VMEM((rank, width // CORES), f32),
            pltpu.SemaphoreType.DMA((2, BLOCKS)),
            pltpu.SemaphoreType.DMA((3,)),
        ],
        compiler_params=params,
        name="finish",
    )(left, p_ortho, q_half, f_half, other, gradient, feedback)
    return (new_feedback, p_ortho, q_factor)


def solution(mesh):
    sizes = (mesh.shape["dp"] // CORES, CORES, math.isqrt(mesh.shape["mp"]), math.isqrt(mesh.shape["mp"]))
    fine = jax.sharding.Mesh(mesh.devices.reshape(sizes), DP + MP)
    return jax.shard_map(
        body,
        mesh=fine,
        in_specs=(P(DP, MP, None), P(DP, MP, None), P()),
        out_specs=(P(DP, MP, None), P(None, MP), P()),
        check_vma=False,
    )
```

```python
import functools
import math

import jax
import jax.numpy as jnp
from jax import lax
from jax.experimental import pallas as pl
from jax.experimental.pallas import tpu as pltpu
from jax.sharding import PartitionSpec as P

LANES = 128
IN_PARTS = 4
IN_TILE = 256
CORES = 2
HALF_GROUPS = 2
BLOCKS = 4
DP = ("x", "core")
MP = ("z", "y")


def dot(left, right, left_dim, right_dim):
    return lax.dot_general(
        left,
        right,
        (((left_dim,), (right_dim,)), ((), ())),
        precision=lax.Precision.HIGHEST,
        preferred_element_type=jnp.float32,
    )


def split(x):
    high = x.astype(jnp.bfloat16)
    rest = x - high.astype(jnp.float32)
    mid = rest.astype(jnp.bfloat16)
    low = (rest - mid.astype(jnp.float32)).astype(jnp.bfloat16)
    return high, mid, low


def bf16_dot(left, right, left_dim, right_dim):
    return lax.dot_general(
        left, right, (((left_dim,), (right_dim,)), ((), ())), preferred_element_type=jnp.float32
    )


def fold(x, size, axis):
    parts = [lax.slice_in_dim(x, n * size, (n + 1) * size, axis=axis) for n in range(3)]
    return (parts[2] + parts[1]) + parts[0]


def correct_kernel(g_hbm, f_hbm, q_hbm, p_ref, c_hbm, g_buf, f_buf, q_buf, c_buf, sems, c_sems):
    half = c_buf.shape[1]
    parts = IN_PARTS // CORES
    width = half // parts
    core = half_of_core()
    copies = []
    for s in range(IN_PARTS):
        first = (1 - core if s < parts else core) * half + s % parts * width
        there = pl.ds(pl.multiple_of(first, width), width)
        here = pl.ds(s * width, width)
        part = [
            pltpu.make_async_copy(g_hbm.at[0, :, there], g_buf.at[:, here], sems.at[0, s]),
            pltpu.make_async_copy(f_hbm.at[0, :, there], f_buf.at[:, here], sems.at[1, s]),
            pltpu.make_async_copy(q_hbm.at[:, there], q_buf.at[:, here], sems.at[2, s]),
        ]
        for copy in part:
            copy.start()
        copies.append(part)
    total = None
    sends = []
    for s in range(IN_PARTS):
        for copy in copies[s]:
            copy.wait()
        for at in range(s * width, (s + 1) * width, IN_TILE):
            cols = slice(at, at + IN_TILE)
            local = g_buf[:, cols] + f_buf[:, cols]
            if s < parts:
                c_buf[:, cols] = local
            left = jnp.concatenate(split(q_buf[:, cols]), axis=0)
            right = jnp.concatenate(split(local), axis=0)
            part = bf16_dot(left, right, 1, 1)
            total = part if total is None else total + part
        if s < parts:
            cols = pl.ds(s * width, width)
            sends.append(pltpu.make_async_copy(c_buf.at[:, cols], c_hbm.at[:, cols], c_sems.at[s]))
            sends[-1].start()
    total = fold(fold(total, total.shape[0] // 3, 0), total.shape[1] // 3, 1)
    half = total.shape[0] // 2
    packed = jnp.concatenate([total[:half], total[half:]], axis=1)
    p_ref[...] = jnp.broadcast_to(packed[None], p_ref.shape)
    for copy in sends:
        copy.wait()


def chip_groups(sizes):
    nx, nc, nz, ny = sizes
    groups = []
    for group in range(nc):
        for half in ((2, 3), (1, 0)):
            groups.append([
                ((x * nc + (group ^ int((x, z, y) == (2, 2, 2)))) * nz + z) * ny + y
                for x in half
                for z in (2, 1, 3, 0)
                for y in (2, 1, 0, 3)
            ])
    groups[2][0], groups[2][8] = groups[2][8], groups[2][0]
    return groups


def half_of_core():
    core = lax.axis_index("core")
    leads = (lax.axis_index("x") == 2) & (lax.axis_index("z") == 2) & (lax.axis_index("y") == 2)
    return jnp.where(leads, 1 - core, core)


def column_at(core, block, width):
    return pl.multiple_of((core * BLOCKS + block) * width, width)


def first_row(block, rank, tiles, length):
    per_group = BLOCKS // HALF_GROUPS
    return block // per_group * rank * length + block % per_group * tiles


def project_kernel(p_ref, g_ref, f_ref, arrived_ref, msg_ref, mean_ref):
    replicas = p_ref.shape[0]
    total = p_ref[0]
    for n in range(1, replicas):
        total = total + p_ref[n]
    total = total * (1.0 / replicas)
    half = total.shape[1] // 2
    mean = jnp.concatenate([total[:, :half], total[:, half:]], axis=0)
    mean_ref[...] = mean
    rank = mean.shape[0]
    high, mid, low = split(mean)
    none = jnp.zeros_like(high)
    left = jnp.concatenate(
        [jnp.concatenate(parts, axis=1) for parts in ((high, high, high), (mid, mid, none), (low, none, none))], axis=0
    )
    width = arrived_ref.shape[1] // BLOCKS
    tiles = width // LANES
    length = BLOCKS // HALF_GROUPS * tiles + 1
    for n in range(BLOCKS):
        cols = pl.ds(column_at(half_of_core(), n, width), width)
        pair = (g_ref[0, :, cols] + f_ref[0, :, cols]) + arrived_ref[:, n * width : (n + 1) * width]
        out = fold(bf16_dot(left, jnp.concatenate(split(pair), axis=0), 1, 0), rank, 0)
        for i in range(tiles):
            first = first_row(n, rank, tiles, length) + i
            for at in (first, first + msg_ref.shape[0] // 2):
                msg_ref[pl.ds(at, rank, stride=length), :] = out[:, i * LANES : (i + 1) * LANES]
    gram = dot(mean, jnp.concatenate([mean] * (LANES // rank), axis=0), 1, 1)
    share = rank // HALF_GROUPS
    row = lax.broadcasted_iota(jnp.int32, (rank, LANES), 0)
    lane = lax.broadcasted_iota(jnp.int32, (rank, LANES), 1)
    mine = row - share * jnp.where((lax.axis_index("x") == 3) | (lax.axis_index("x") == 0), 1, 0)
    kept = (lane >= rank * mine) & (lane < rank * (mine + 1)) & (mine >= 0) & (mine < share)
    line = jnp.sum(jnp.where(kept, gram, 0.0), axis=0, keepdims=True)
    count = msg_ref.shape[0] // length
    msg_ref[pl.ds(length - 1, count, stride=length), :] = jnp.broadcast_to(line, (count, LANES))


def sum_kernel(in_ref, out_ref, gram_ref, part):
    members = HALF_GROUPS * gram_ref.shape[0]
    length = in_ref.shape[0] // (2 * members)
    rows = part.shape[0]
    total = in_ref[0:rows]
    for s in range(1, in_ref.shape[0] // rows):
        total = total + in_ref[rows * s : rows * (s + 1)]
    part[...] = total
    copies = out_ref.shape[0] // (length - 1)
    for i in range(length - 1):
        line = jnp.sum(part[pl.ds(i, rows // length, stride=length), :], axis=0, keepdims=True)
        out_ref[pl.ds(i, copies, stride=length - 1), :] = jnp.broadcast_to(line, (copies, LANES))
    shards = members // HALF_GROUPS
    share = gram_ref.shape[0] // HALF_GROUPS
    for n in range(HALF_GROUPS):
        terms = in_ref[pl.ds(n * shards * length + length - 1, shards, stride=length), :]
        line = jnp.sum(terms, axis=0, keepdims=True)
        gram_ref[n * share : (n + 1) * share, :] = jnp.broadcast_to(line, (share, LANES))


def inverse_factor(spread):
    rank = spread.shape[0]
    share = rank // HALF_GROUPS
    row = lax.broadcasted_iota(jnp.int32, (rank, LANES), 0)
    lane = lax.broadcasted_iota(jnp.int32, (rank, LANES), 1)
    at = lane - rank * (row % share)
    cols = [
        jnp.broadcast_to(jnp.sum(jnp.where(at == j, spread, 0.0), axis=1, keepdims=True), (rank, LANES))
        for j in range(rank)
    ]
    right = jnp.where(row == lane, 1.0, 0.0)
    pivots = jnp.ones((rank, LANES), jnp.float32)
    for k in range(rank):
        pivot = cols[k][k : k + 1]
        pivots = jnp.where(row == k, pivot, pivots)
        factor = jnp.where(row > k, cols[k] * (1.0 / pivot), 0.0)
        for j in range(k + 1, rank):
            cols[j] = cols[j] - factor * cols[j][k : k + 1]
        right = right - factor * right[k : k + 1]
    return right * (1.0 / jnp.sqrt(pivots))


def half_block(left, half_ref, g_ref, f_ref, core, n, rank):
    width = g_ref.shape[2] // CORES // BLOCKS
    tiles = width // LANES
    length = BLOCKS // HALF_GROUPS * tiles
    first = first_row(n, rank, tiles, length)
    raw = jnp.concatenate([half_ref[pl.ds(first + i, rank, stride=length), :] for i in range(tiles)], axis=1)
    high, mid, low = split(raw)
    out = bf16_dot(left, jnp.concatenate([high, mid, high, low, high, mid], axis=0), 1, 0)
    cols = pl.ds(column_at(core, n, width), width)
    return out[:rank], (g_ref[0, :, cols] + f_ref[0, :, cols]) - out[rank:]


def own_half_kernel(replicas, gram_ref, half_ref, mean_ref, g_ref, f_ref, left_ref, po_ref, qf_ref, nf_ref):
    rank = mean_ref.shape[0]
    whole = inverse_factor(gram_ref[...])
    lower = whole[:, :rank]
    ortho = dot(lower, mean_ref[...], 1, 0)
    po_ref[...] = ortho
    scaled = lower * (1.0 / replicas)
    both = jnp.concatenate([scaled, dot(ortho, scaled, 0, 0)], axis=0)
    high, mid, low = split(both)
    left = jnp.concatenate([high, high, mid, high, low, mid], axis=1)
    left_ref[...] = left
    width = qf_ref.shape[1] // BLOCKS
    core = half_of_core()
    for n in range(BLOCKS):
        cols = slice(n * width, (n + 1) * width)
        qf_ref[:, cols], nf_ref[:, cols] = half_block(left, half_ref, g_ref, f_ref, core, n, rank)


def finish_kernel(
    left_ref, po_ref, qf_ref, nf_ref, half_ref, g_ref, f_ref, nf_hbm, po_hbm, qf_hbm, nf_buf, qf_buf, sems, half_sems
):
    rank = po_ref.shape[0]
    core = half_of_core()
    width = qf_ref.shape[1] // BLOCKS
    own = pl.ds(column_at(core, 0, width), BLOCKS * width)
    copies = [
        pltpu.make_async_copy(nf_ref, nf_hbm.at[0, :, own], half_sems.at[0]),
        pltpu.make_async_copy(qf_ref, qf_hbm.at[:, own], half_sems.at[1]),
        pltpu.make_async_copy(po_ref, po_hbm, half_sems.at[2]),
    ]
    for copy in copies:
        copy.start()
    left = left_ref[...]
    for n in range(BLOCKS):
        cols = slice(n * width, (n + 1) * width)
        qf_buf[:, cols], nf_buf[:, cols] = half_block(left, half_ref, g_ref, f_ref, 1 - core, n, rank)
        here = pl.ds(n * width, width)
        there = pl.ds(column_at(1 - core, n, width), width)
        part = [
            pltpu.make_async_copy(nf_buf.at[:, here], nf_hbm.at[0, :, there], sems.at[0, n]),
            pltpu.make_async_copy(qf_buf.at[:, here], qf_hbm.at[:, there], sems.at[1, n]),
        ]
        for copy in part:
            copy.start()
        copies += part
    for copy in copies:
        copy.wait()


def body(gradient, feedback, q_previous):
    f32 = jnp.float32
    dp, mp = lax.axis_size(DP), lax.axis_size(MP)
    _, rows, width = gradient.shape
    rank = q_previous.shape[0]
    tiles = width // CORES // HALF_GROUPS // LANES
    members = HALF_GROUPS * rank
    vmem = pl.BlockSpec(memory_space=pltpu.VMEM)
    hbm = pl.BlockSpec(memory_space=pltpu.HBM)
    params = pltpu.CompilerParams(vmem_limit_bytes=16 * 2**20)

    p_out, c_send = pl.pallas_call(
        correct_kernel,
        in_specs=[hbm, hbm, hbm],
        out_specs=[vmem, hbm],
        out_shape=[
            jax.ShapeDtypeStruct((dp, rank // 2, 2 * rows), f32),
            jax.ShapeDtypeStruct((rows, width // CORES), f32),
        ],
        scratch_shapes=[
            pltpu.VMEM((rows, width), f32),
            pltpu.VMEM((rows, width), f32),
            pltpu.VMEM((rank, width), f32),
            pltpu.VMEM((rows, width // CORES), f32),
            pltpu.SemaphoreType.DMA((3, IN_PARTS)),
            pltpu.SemaphoreType.DMA((IN_PARTS // CORES,)),
        ],
        compiler_params=pltpu.CompilerParams(vmem_limit_bytes=int(53.75 * 2**20)),
        name="correct",
    )(gradient, feedback, q_previous)
    sizes = tuple(lax.axis_size(name) for name in DP + MP)
    near = [[x * CORES + core for x in (2, 1, 0, 3) for core in (0, 1)]]
    halves = chip_groups(sizes)
    chips = [halves[2 * n] + halves[2 * n + 1] for n in range(CORES)]
    arrived = lax.ppermute(c_send, "core", [(0, 1), (1, 0)])
    p_all = lax.all_to_all(p_out, DP, 0, 0, tiled=True, axis_index_groups=near)

    count = sizes[0] * mp
    msg, p_mean = pl.pallas_call(
        project_kernel,
        in_specs=[vmem] * 4,
        out_specs=[vmem] * 2,
        out_shape=[
            jax.ShapeDtypeStruct((count * (tiles + 1), LANES), f32),
            jax.ShapeDtypeStruct((rank, rows), f32),
        ],
        compiler_params=params,
        name="project",
    )(p_all, gradient, feedback, arrived)
    msg = msg.reshape(count, 1, (tiles + 1) * LANES)
    terms = lax.all_to_all(msg, DP + MP, 0, 0, tiled=True, axis_index_groups=chips)

    own, gram = pl.pallas_call(
        sum_kernel,
        in_specs=[vmem],
        out_specs=[vmem, vmem],
        out_shape=[
            jax.ShapeDtypeStruct((members * tiles, LANES), f32),
            jax.ShapeDtypeStruct((rank, LANES), f32),
        ],
        scratch_shapes=[pltpu.VMEM((8 * (tiles + 1), LANES), f32)],
        compiler_params=params,
        name="sum_terms",
    )(terms.reshape(count * (tiles + 1), LANES))
    own = own.reshape(members, 1, tiles * LANES)
    half = lax.all_to_all(own, DP + MP, 0, 0, tiled=True, axis_index_groups=halves).reshape(members * tiles, LANES)
    other = lax.ppermute(half, "core", [(0, 1), (1, 0)])

    left, p_ortho, q_half, f_half = pl.pallas_call(
        functools.partial(own_half_kernel, dp),
        in_specs=[vmem] * 5,
        out_specs=[vmem] * 4,
        out_shape=[
            jax.ShapeDtypeStruct((rank + rows, 6 * rank), jnp.bfloat16),
            jax.ShapeDtypeStruct((rank, rows), f32),
            jax.ShapeDtypeStruct((rank, width // CORES), f32),
            jax.ShapeDtypeStruct((rows, width // CORES), f32),
        ],
        compiler_params=params,
        cost_estimate=pl.CostEstimate(flops=2 * rows * width * 96, bytes_accessed=8 * rows * width, transcendentals=0),
        name="own_half",
    )(gram, half, p_mean, gradient, feedback)
    new_feedback, p_ortho, q_factor = pl.pallas_call(
        finish_kernel,
        in_specs=[vmem] * 7,
        out_specs=[hbm] * 3,
        out_shape=[
            jax.ShapeDtypeStruct((1, rows, width), f32),
            jax.ShapeDtypeStruct((rank, rows), f32),
            jax.ShapeDtypeStruct((rank, width), f32),
        ],
        scratch_shapes=[
            pltpu.VMEM((rows, width // CORES), f32),
            pltpu.VMEM((rank, width // CORES), f32),
            pltpu.SemaphoreType.DMA((2, BLOCKS)),
            pltpu.SemaphoreType.DMA((3,)),
        ],
        compiler_params=params,
        name="finish",
    )(left, p_ortho, q_half, f_half, other, gradient, feedback)
    return (new_feedback, p_ortho, q_factor)


def solution(mesh):
    sizes = (mesh.shape["dp"] // CORES, CORES, math.isqrt(mesh.shape["mp"]), math.isqrt(mesh.shape["mp"]))
    fine = jax.sharding.Mesh(mesh.devices.reshape(sizes), DP + MP)
    return jax.shard_map(
        body,
        mesh=fine,
        in_specs=(P(DP, MP, None), P(DP, MP, None), P()),
        out_specs=(P(DP, MP, None), P(None, MP), P()),
        check_vma=False,
    )
```

```python
import functools
import math

import jax
import jax.numpy as jnp
from jax import lax
from jax.experimental import pallas as pl
from jax.experimental.pallas import tpu as pltpu
from jax.sharding import PartitionSpec as P

LANES = 128
IN_PARTS = 4
IN_TILE = 256
CORES = 2
HALF_GROUPS = 2
BLOCKS = 4
DP = ("x", "core")
MP = ("z", "y")


def dot(left, right, left_dim, right_dim):
    return lax.dot_general(
        left,
        right,
        (((left_dim,), (right_dim,)), ((), ())),
        precision=lax.Precision.HIGHEST,
        preferred_element_type=jnp.float32,
    )


def split(x):
    high = x.astype(jnp.bfloat16)
    rest = x - high.astype(jnp.float32)
    mid = rest.astype(jnp.bfloat16)
    low = (rest - mid.astype(jnp.float32)).astype(jnp.bfloat16)
    return high, mid, low


def bf16_dot(left, right, left_dim, right_dim):
    return lax.dot_general(
        left, right, (((left_dim,), (right_dim,)), ((), ())), preferred_element_type=jnp.float32
    )


def fold(x, size, axis):
    parts = [lax.slice_in_dim(x, n * size, (n + 1) * size, axis=axis) for n in range(3)]
    return (parts[2] + parts[1]) + parts[0]


def correct_kernel(g_hbm, f_hbm, q_hbm, p_ref, c_hbm, g_buf, f_buf, q_buf, c_buf, sems, c_sems):
    half = c_buf.shape[1]
    parts = IN_PARTS // CORES
    width = half // parts
    core = half_of_core()
    copies = []
    for s in range(IN_PARTS):
        first = (1 - core if s < parts else core) * half + s % parts * width
        there = pl.ds(pl.multiple_of(first, width), width)
        here = pl.ds(s * width, width)
        part = [
            pltpu.make_async_copy(g_hbm.at[0, :, there], g_buf.at[:, here], sems.at[0, s]),
            pltpu.make_async_copy(f_hbm.at[0, :, there], f_buf.at[:, here], sems.at[1, s]),
            pltpu.make_async_copy(q_hbm.at[:, there], q_buf.at[:, here], sems.at[2, s]),
        ]
        for copy in part:
            copy.start()
        copies.append(part)
    total = None
    sends = []
    for s in range(IN_PARTS):
        for copy in copies[s]:
            copy.wait()
        for at in range(s * width, (s + 1) * width, IN_TILE):
            cols = slice(at, at + IN_TILE)
            local = g_buf[:, cols] + f_buf[:, cols]
            if s < parts:
                c_buf[:, cols] = local
            left = jnp.concatenate(split(q_buf[:, cols]), axis=0)
            right = jnp.concatenate(split(local), axis=0)
            part = bf16_dot(left, right, 1, 1)
            total = part if total is None else total + part
        if s < parts:
            cols = pl.ds(s * width, width)
            sends.append(pltpu.make_async_copy(c_buf.at[:, cols], c_hbm.at[:, cols], c_sems.at[s]))
            sends[-1].start()
    total = fold(fold(total, total.shape[0] // 3, 0), total.shape[1] // 3, 1)
    half = total.shape[0] // 2
    packed = jnp.concatenate([total[:half], total[half:]], axis=1)
    p_ref[...] = jnp.broadcast_to(packed[None], p_ref.shape)
    for copy in sends:
        copy.wait()


def chip_groups(sizes):
    nx, nc, nz, ny = sizes
    groups = []
    for group in range(nc):
        for half in ((2, 3), (1, 0)):
            groups.append([
                ((x * nc + (group ^ int((x, z, y) in ((2, 2, 2), (1, 2, 2))))) * nz + z) * ny + y
                for x in half
                for z in (2, 1, 3, 0)
                for y in (2, 1, 0, 3)
            ])
    groups[2][0], groups[2][8] = groups[2][8], groups[2][0]
    return groups


def half_of_core():
    core = lax.axis_index("core")
    leads = ((lax.axis_index("x") == 2) | (lax.axis_index("x") == 1)) & (lax.axis_index("z") == 2) & (lax.axis_index("y") == 2)
    return jnp.where(leads, 1 - core, core)


def column_at(core, block, width):
    return pl.multiple_of((core * BLOCKS + block) * width, width)


def first_row(block, rank, tiles, length):
    per_group = BLOCKS // HALF_GROUPS
    return block // per_group * rank * length + block % per_group * tiles


def project_kernel(p_ref, g_ref, f_ref, arrived_ref, msg_ref, mean_ref):
    replicas = p_ref.shape[0]
    total = p_ref[0]
    for n in range(1, replicas):
        total = total + p_ref[n]
    total = total * (1.0 / replicas)
    half = total.shape[1] // 2
    mean = jnp.concatenate([total[:, :half], total[:, half:]], axis=0)
    mean_ref[...] = mean
    rank = mean.shape[0]
    high, mid, low = split(mean)
    none = jnp.zeros_like(high)
    left = jnp.concatenate(
        [jnp.concatenate(parts, axis=1) for parts in ((high, high, high), (mid, mid, none), (low, none, none))], axis=0
    )
    width = arrived_ref.shape[1] // BLOCKS
    tiles = width // LANES
    length = BLOCKS // HALF_GROUPS * tiles + 1
    for n in range(BLOCKS):
        cols = pl.ds(column_at(half_of_core(), n, width), width)
        pair = (g_ref[0, :, cols] + f_ref[0, :, cols]) + arrived_ref[:, n * width : (n + 1) * width]
        out = fold(bf16_dot(left, jnp.concatenate(split(pair), axis=0), 1, 0), rank, 0)
        for i in range(tiles):
            first = first_row(n, rank, tiles, length) + i
            for at in (first, first + msg_ref.shape[0] // 2):
                msg_ref[pl.ds(at, rank, stride=length), :] = out[:, i * LANES : (i + 1) * LANES]
    gram = dot(mean, jnp.concatenate([mean] * (LANES // rank), axis=0), 1, 1)
    share = rank // HALF_GROUPS
    row = lax.broadcasted_iota(jnp.int32, (rank, LANES), 0)
    lane = lax.broadcasted_iota(jnp.int32, (rank, LANES), 1)
    mine = row - share * jnp.where((lax.axis_index("x") == 3) | (lax.axis_index("x") == 0), 1, 0)
    kept = (lane >= rank * mine) & (lane < rank * (mine + 1)) & (mine >= 0) & (mine < share)
    line = jnp.sum(jnp.where(kept, gram, 0.0), axis=0, keepdims=True)
    count = msg_ref.shape[0] // length
    msg_ref[pl.ds(length - 1, count, stride=length), :] = jnp.broadcast_to(line, (count, LANES))


def sum_kernel(in_ref, out_ref, gram_ref, part):
    members = HALF_GROUPS * gram_ref.shape[0]
    length = in_ref.shape[0] // (2 * members)
    rows = part.shape[0]
    total = in_ref[0:rows]
    for s in range(1, in_ref.shape[0] // rows):
        total = total + in_ref[rows * s : rows * (s + 1)]
    part[...] = total
    copies = out_ref.shape[0] // (length - 1)
    for i in range(length - 1):
        line = jnp.sum(part[pl.ds(i, rows // length, stride=length), :], axis=0, keepdims=True)
        out_ref[pl.ds(i, copies, stride=length - 1), :] = jnp.broadcast_to(line, (copies, LANES))
    shards = members // HALF_GROUPS
    share = gram_ref.shape[0] // HALF_GROUPS
    for n in range(HALF_GROUPS):
        terms = in_ref[pl.ds(n * shards * length + length - 1, shards, stride=length), :]
        line = jnp.sum(terms, axis=0, keepdims=True)
        gram_ref[n * share : (n + 1) * share, :] = jnp.broadcast_to(line, (share, LANES))


def inverse_factor(spread):
    rank = spread.shape[0]
    share = rank // HALF_GROUPS
    row = lax.broadcasted_iota(jnp.int32, (rank, LANES), 0)
    lane = lax.broadcasted_iota(jnp.int32, (rank, LANES), 1)
    at = lane - rank * (row % share)
    cols = [
        jnp.broadcast_to(jnp.sum(jnp.where(at == j, spread, 0.0), axis=1, keepdims=True), (rank, LANES))
        for j in range(rank)
    ]
    right = jnp.where(row == lane, 1.0, 0.0)
    pivots = jnp.ones((rank, LANES), jnp.float32)
    for k in range(rank):
        pivot = cols[k][k : k + 1]
        pivots = jnp.where(row == k, pivot, pivots)
        factor = jnp.where(row > k, cols[k] * (1.0 / pivot), 0.0)
        for j in range(k + 1, rank):
            cols[j] = cols[j] - factor * cols[j][k : k + 1]
        right = right - factor * right[k : k + 1]
    return right * (1.0 / jnp.sqrt(pivots))


def half_block(left, half_ref, g_ref, f_ref, core, n, rank):
    width = g_ref.shape[2] // CORES // BLOCKS
    tiles = width // LANES
    length = BLOCKS // HALF_GROUPS * tiles
    first = first_row(n, rank, tiles, length)
    raw = jnp.concatenate([half_ref[pl.ds(first + i, rank, stride=length), :] for i in range(tiles)], axis=1)
    high, mid, low = split(raw)
    out = bf16_dot(left, jnp.concatenate([high, mid, high, low, high, mid], axis=0), 1, 0)
    cols = pl.ds(column_at(core, n, width), width)
    return out[:rank], (g_ref[0, :, cols] + f_ref[0, :, cols]) - out[rank:]


def own_half_kernel(replicas, gram_ref, half_ref, mean_ref, g_ref, f_ref, left_ref, po_ref, qf_ref, nf_ref):
    rank = mean_ref.shape[0]
    whole = inverse_factor(gram_ref[...])
    lower = whole[:, :rank]
    ortho = dot(lower, mean_ref[...], 1, 0)
    po_ref[...] = ortho
    scaled = lower * (1.0 / replicas)
    both = jnp.concatenate([scaled, dot(ortho, scaled, 0, 0)], axis=0)
    high, mid, low = split(both)
    left = jnp.concatenate([high, high, mid, high, low, mid], axis=1)
    left_ref[...] = left
    width = qf_ref.shape[1] // BLOCKS
    core = half_of_core()
    for n in range(BLOCKS):
        cols = slice(n * width, (n + 1) * width)
        qf_ref[:, cols], nf_ref[:, cols] = half_block(left, half_ref, g_ref, f_ref, core, n, rank)


def finish_kernel(
    left_ref, po_ref, qf_ref, nf_ref, half_ref, g_ref, f_ref, nf_hbm, po_hbm, qf_hbm, nf_buf, qf_buf, sems, half_sems
):
    rank = po_ref.shape[0]
    core = half_of_core()
    width = qf_ref.shape[1] // BLOCKS
    own = pl.ds(column_at(core, 0, width), BLOCKS * width)
    copies = [
        pltpu.make_async_copy(nf_ref, nf_hbm.at[0, :, own], half_sems.at[0]),
        pltpu.make_async_copy(qf_ref, qf_hbm.at[:, own], half_sems.at[1]),
        pltpu.make_async_copy(po_ref, po_hbm, half_sems.at[2]),
    ]
    for copy in copies:
        copy.start()
    left = left_ref[...]
    for n in range(BLOCKS):
        cols = slice(n * width, (n + 1) * width)
        qf_buf[:, cols], nf_buf[:, cols] = half_block(left, half_ref, g_ref, f_ref, 1 - core, n, rank)
        here = pl.ds(n * width, width)
        there = pl.ds(column_at(1 - core, n, width), width)
        part = [
            pltpu.make_async_copy(nf_buf.at[:, here], nf_hbm.at[0, :, there], sems.at[0, n]),
            pltpu.make_async_copy(qf_buf.at[:, here], qf_hbm.at[:, there], sems.at[1, n]),
        ]
        for copy in part:
            copy.start()
        copies += part
    for copy in copies:
        copy.wait()


def body(gradient, feedback, q_previous):
    f32 = jnp.float32
    dp, mp = lax.axis_size(DP), lax.axis_size(MP)
    _, rows, width = gradient.shape
    rank = q_previous.shape[0]
    tiles = width // CORES // HALF_GROUPS // LANES
    members = HALF_GROUPS * rank
    vmem = pl.BlockSpec(memory_space=pltpu.VMEM)
    hbm = pl.BlockSpec(memory_space=pltpu.HBM)
    params = pltpu.CompilerParams(vmem_limit_bytes=16 * 2**20)

    p_out, c_send = pl.pallas_call(
        correct_kernel,
        in_specs=[hbm, hbm, hbm],
        out_specs=[vmem, hbm],
        out_shape=[
            jax.ShapeDtypeStruct((dp, rank // 2, 2 * rows), f32),
            jax.ShapeDtypeStruct((rows, width // CORES), f32),
        ],
        scratch_shapes=[
            pltpu.VMEM((rows, width), f32),
            pltpu.VMEM((rows, width), f32),
            pltpu.VMEM((rank, width), f32),
            pltpu.VMEM((rows, width // CORES), f32),
            pltpu.SemaphoreType.DMA((3, IN_PARTS)),
            pltpu.SemaphoreType.DMA((IN_PARTS // CORES,)),
        ],
        compiler_params=pltpu.CompilerParams(vmem_limit_bytes=int(53.75 * 2**20)),
        name="correct",
    )(gradient, feedback, q_previous)
    sizes = tuple(lax.axis_size(name) for name in DP + MP)
    near = [[x * CORES + core for x in (2, 1, 0, 3) for core in (0, 1)]]
    halves = chip_groups(sizes)
    chips = [halves[2 * n] + halves[2 * n + 1] for n in range(CORES)]
    arrived = lax.ppermute(c_send, "core", [(0, 1), (1, 0)])
    p_all = lax.all_to_all(p_out, DP, 0, 0, tiled=True, axis_index_groups=near)

    count = sizes[0] * mp
    msg, p_mean = pl.pallas_call(
        project_kernel,
        in_specs=[vmem] * 4,
        out_specs=[vmem] * 2,
        out_shape=[
            jax.ShapeDtypeStruct((count * (tiles + 1), LANES), f32),
            jax.ShapeDtypeStruct((rank, rows), f32),
        ],
        compiler_params=params,
        name="project",
    )(p_all, gradient, feedback, arrived)
    msg = msg.reshape(count, 1, (tiles + 1) * LANES)
    terms = lax.all_to_all(msg, DP + MP, 0, 0, tiled=True, axis_index_groups=chips)

    own, gram = pl.pallas_call(
        sum_kernel,
        in_specs=[vmem],
        out_specs=[vmem, vmem],
        out_shape=[
            jax.ShapeDtypeStruct((members * tiles, LANES), f32),
            jax.ShapeDtypeStruct((rank, LANES), f32),
        ],
        scratch_shapes=[pltpu.VMEM((8 * (tiles + 1), LANES), f32)],
        compiler_params=params,
        name="sum_terms",
    )(terms.reshape(count * (tiles + 1), LANES))
    own = own.reshape(members, 1, tiles * LANES)
    half = lax.all_to_all(own, DP + MP, 0, 0, tiled=True, axis_index_groups=halves).reshape(members * tiles, LANES)
    other = lax.ppermute(half, "core", [(0, 1), (1, 0)])

    left, p_ortho, q_half, f_half = pl.pallas_call(
        functools.partial(own_half_kernel, dp),
        in_specs=[vmem] * 5,
        out_specs=[vmem] * 4,
        out_shape=[
            jax.ShapeDtypeStruct((rank + rows, 6 * rank), jnp.bfloat16),
            jax.ShapeDtypeStruct((rank, rows), f32),
            jax.ShapeDtypeStruct((rank, width // CORES), f32),
            jax.ShapeDtypeStruct((rows, width // CORES), f32),
        ],
        compiler_params=params,
        cost_estimate=pl.CostEstimate(flops=2 * rows * width * 96, bytes_accessed=8 * rows * width, transcendentals=0),
        name="own_half",
    )(gram, half, p_mean, gradient, feedback)
    new_feedback, p_ortho, q_factor = pl.pallas_call(
        finish_kernel,
        in_specs=[vmem] * 7,
        out_specs=[hbm] * 3,
        out_shape=[
            jax.ShapeDtypeStruct((1, rows, width), f32),
            jax.ShapeDtypeStruct((rank, rows), f32),
            jax.ShapeDtypeStruct((rank, width), f32),
        ],
        scratch_shapes=[
            pltpu.VMEM((rows, width // CORES), f32),
            pltpu.VMEM((rank, width // CORES), f32),
            pltpu.SemaphoreType.DMA((2, BLOCKS)),
            pltpu.SemaphoreType.DMA((3,)),
        ],
        compiler_params=params,
        name="finish",
    )(left, p_ortho, q_half, f_half, other, gradient, feedback)
    return (new_feedback, p_ortho, q_factor)


def solution(mesh):
    sizes = (mesh.shape["dp"] // CORES, CORES, math.isqrt(mesh.shape["mp"]), math.isqrt(mesh.shape["mp"]))
    fine = jax.sharding.Mesh(mesh.devices.reshape(sizes), DP + MP)
    return jax.shard_map(
        body,
        mesh=fine,
        in_specs=(P(DP, MP, None), P(DP, MP, None), P()),
        out_specs=(P(DP, MP, None), P(None, MP), P()),
        check_vma=False,
    )
```
